512 devices in a mesh: seq: 128 (over z, y, core), head: 4 (over x).
Axes of the slice: x: 4, y: 8, z: 8, core: 2. Of those that a mesh axis runs over, the one named last changes fastest.
Arguments:
- features: bfloat16 [256, 131072], P('head', 'seq'), as said below
- neighbours: int32 [2, 27, 131072], P(None, None, 'seq'), may hold values from -1 to 131071, as said below
- valid: int32 [2, 131072], P(None, 'seq'), may hold values from 0 to 1, as said below
- conv_weight: bfloat16 [2, 27, 256, 256], P(None, None, 'head'), may hold values from -0.078125 to 0.078125
- attn_weight: bfloat16 [2, 3, 256, 256], P(None, None, 'head'), as said below
- proj_weight: bfloat16 [2, 256, 256], P(None, 'head'), may hold values from -0.375 to 0.375
- hilbert_place: int32 [131072], P('seq'), may hold values from 0 to 131071, as said below
Outputs:
- output: bfloat16 [256, 131072], P('head', 'seq')
The draws below stay inside these ranges and needn't reach their ends.
Inputs may be any that keep to these rules, and one draw needn't show every extreme that they name: `neighbours`: each entry is -1 or the index of a point within 256 positions of the point itself; tap 13 is always the point itself. The first point of every patch is valid. `hilbert_place`: A permutation of all points. Of the points on one index of seq, at most 16 go to any one index of seq in Hilbert order, and in every draw some go exactly 16; they go to 96 indices. `features`: values within -6 to 6. `attn_weight`: values within -0.2 to 0.2 at the stated sizes.
All inputs are finite; a program needn't handle non-finite values.
Results may differ from the reference program's by a relative error of at most 0.015.
Values may be sent and summed in bfloat16 or wider, within the bound.
A program may use at most 64 MiB of HBM per device.

```python
import jax
import jax.numpy as jnp
from jax import lax

C = 256
HEADS = 16
PATCH = 1024
TOK_DEV = 1024
HD = 16
POINTS = 131072
REACH = 256
CAP = 16
PIECES = 96


def draw_features(key, part):
    key = jax.random.fold_in(key, 1)
    first_key = jax.random.fold_in(key, 0)
    values = jax.random.truncated_normal(first_key, -4.0, 4.0, (POINTS, C), jnp.float32)
    return values.T.astype(jnp.bfloat16)


def draw_attn_weight(key, part):
    key = jax.random.fold_in(key, 2)
    first_key = jax.random.fold_in(key, 0)
    factor = C ** (-0.5)
    values = jax.random.truncated_normal(first_key, -3.0, 3.0, (2, 3, C, C), jnp.float32) * factor
    return values.astype(jnp.bfloat16)


def draw_neighbours(key, part):
    key = jax.random.fold_in(key, 3)
    first_key, second_key = jax.random.split(key, 2)
    offsets = jax.random.randint(first_key, (2, POINTS, 27), -REACH, REACH + 1)
    keep = jax.random.randint(second_key, (2, POINTS, 27), 0, 10) < 7
    centre = (jnp.arange(27, dtype=jnp.int32) == 13)[None, None, :]
    offsets = jnp.where(centre, 0, offsets)
    keep = keep | centre
    target = jnp.arange(POINTS, dtype=jnp.int32)[None, :, None] + offsets
    good = keep & (target >= 0) & (target < POINTS)
    return jnp.transpose(jnp.where(good, target, -1), (0, 2, 1)).astype(jnp.int32)


def draw_valid(key, part):
    key = jax.random.fold_in(key, 4)
    live = jax.random.randint(key, (2, POINTS), 0, 4) > 0
    heads = (jnp.arange(POINTS, dtype=jnp.int32) % PATCH == 0)[None, :]
    return (live | heads).astype(jnp.int32)


def draw_hilbert_place(key, part):
    key = jax.random.fold_in(key, 5)
    keys = jax.random.split(key, 5)
    shards = POINTS // TOK_DEV
    groups = PIECES // 3
    middle = jax.random.randint(keys[0], (groups,), 1, CAP)
    sizes = jnp.stack([jnp.full((groups,), CAP, jnp.int32), middle, CAP - middle], axis=1).reshape(PIECES)
    ends = jnp.cumsum(sizes)
    shuffled = jax.random.permutation(keys[1], shards).astype(jnp.int32)
    ranking = jnp.where(shuffled == shards // 2, -1, jnp.arange(shards, dtype=jnp.int32))
    shifts = shuffled[jnp.argsort(ranking)][:PIECES].astype(jnp.int32)
    slot = jnp.arange(TOK_DEV, dtype=jnp.int32)
    piece = jnp.sum((slot[:, None] >= ends[None, :]).astype(jnp.int32), axis=1)
    source_order = jax.vmap(lambda k: jax.random.permutation(k, TOK_DEV))(jax.random.split(keys[3], shards)).astype(jnp.int32)
    target_order = jax.vmap(lambda k: jax.random.permutation(k, TOK_DEV))(jax.random.split(keys[4], shards)).astype(jnp.int32)
    device = jnp.arange(shards, dtype=jnp.int32)[:, None]
    target_device = (device + shifts[piece][None, :]) % shards
    target = target_device * TOK_DEV + target_order[target_device, slot[None, :]]
    places = jnp.zeros((shards, TOK_DEV), jnp.int32).at[jnp.broadcast_to(device, (shards, TOK_DEV)), source_order].set(target)
    return places.reshape(POINTS).astype(jnp.int32)


def steps_of(own_key, dims, cuts, low, top_value):
    loudness = 1.0
    for dim, parts in cuts:
        heights = jax.random.uniform(jax.random.fold_in(jax.random.fold_in(own_key, 6), dim), (parts,), jnp.float32, low / len(cuts), top_value / len(cuts))
        loudness = loudness * jnp.repeat(jnp.exp(heights), dims[dim] // parts).reshape((-1,) + (1,) * (len(dims) - 1 - dim))
    return loudness


def scatter_about(stream_key, extent, deviation, most, pieces=(), kind=jnp.bfloat16):
    level = steps_of(stream_key, extent, pieces, -0.22, 0.18) if pieces else 1.0
    values = jax.random.normal(stream_key, extent, jnp.float32) * deviation * level
    return jnp.minimum(jnp.maximum(values, -most), most).astype(kind)


def setup_inputs(seed: int = 0) -> dict:
    splits = jax.random.split(jax.random.key(seed), 8)
    features = draw_features(jax.random.fold_in(splits[7], 71), 0)
    neighbours = draw_neighbours(jax.random.fold_in(splits[7], 71), 0)
    valid = draw_valid(jax.random.fold_in(splits[7], 71), 0)
    conv_weight = scatter_about(splits[3], (2, 27, C, C), (27 * C) ** -0.5, 0.078125, ((2, 4),))
    attn_weight = draw_attn_weight(jax.random.fold_in(splits[7], 71), 0)
    proj_weight = scatter_about(splits[5], (2, C, C), C ** -0.5, 0.375, ((1, 4),))
    hilbert_place = draw_hilbert_place(jax.random.fold_in(splits[7], 71), 0)
    return dict(features=features, neighbours=neighbours, valid=valid, conv_weight=conv_weight, attn_weight=attn_weight, proj_weight=proj_weight, hilbert_place=hilbert_place)


def layer_norm(values):
    mean = lax.optimization_barrier(jnp.mean(values, axis=-1, keepdims=True))
    centred = values - mean
    spread = lax.optimization_barrier(jnp.mean(centred * centred, axis=-1, keepdims=True))
    return centred * lax.rsqrt(spread + 1e-05)

def sparse_conv(table, nbrs, weight):

    def step(tap, total):
        index = lax.dynamic_index_in_dim(nbrs, tap, 1, keepdims=False)
        rows = jnp.take(table, jnp.maximum(index, 0), axis=0)
        rows = jnp.where((index >= 0)[:, None], rows, jnp.zeros_like(rows))
        return total + jnp.dot(rows, weight[tap], preferred_element_type=jnp.float32)
    start = jnp.zeros((table.shape[0], weight.shape[2]), jnp.float32)
    return lax.fori_loop(0, 27, step, start)

def run_block(feats, nbrs, mask, conv_w, qkv_w, proj_w):
    mixed = (feats.astype(jnp.float32) + sparse_conv(feats, nbrs, conv_w)).astype(jnp.bfloat16)
    normed = layer_norm(mixed.astype(jnp.float32)).astype(jnp.bfloat16)
    query = jnp.dot(normed, qkv_w[0], preferred_element_type=jnp.float32).astype(jnp.bfloat16)
    keys = jnp.dot(normed, qkv_w[1], preferred_element_type=jnp.float32).astype(jnp.bfloat16)
    values = jnp.dot(normed, qkv_w[2], preferred_element_type=jnp.float32).astype(jnp.bfloat16)
    count = feats.shape[0] // PATCH
    scale = 1.0 / HD ** 0.5

    def one_patch(args):
        qpart, kpart, vpart, mpart = args
        scores = jnp.einsum('qhd,khd->hqk', qpart.astype(jnp.float32), kpart.astype(jnp.float32)) * scale
        scores = jnp.where(mpart[None, None, :] > 0, scores, -1e+30)
        top = lax.optimization_barrier(jnp.max(scores, axis=2, keepdims=True))
        weights = jnp.exp(scores - top)
        total = lax.optimization_barrier(jnp.sum(weights, axis=2, keepdims=True))
        probs = (weights / total).astype(jnp.bfloat16)
        return jnp.einsum('hqk,khd->qhd', probs.astype(jnp.float32), vpart.astype(jnp.float32)).astype(jnp.bfloat16)
    shaped = (query.reshape(count, PATCH, HEADS, HD), keys.reshape(count, PATCH, HEADS, HD), values.reshape(count, PATCH, HEADS, HD), mask.reshape(count, PATCH))
    heads_out = lax.map(one_patch, shaped).reshape(feats.shape[0], C)
    update = jnp.dot(heads_out, proj_w, preferred_element_type=jnp.float32)
    return (mixed.astype(jnp.float32) + update).astype(jnp.bfloat16)

def reference(features, neighbours, valid, conv_weight, attn_weight, proj_weight, hilbert_place):
    feats = features.T
    nbrs = jnp.transpose(neighbours, (0, 2, 1))
    conv_w = jnp.swapaxes(conv_weight, 2, 3)
    qkv_w = jnp.swapaxes(attn_weight, 2, 3)
    first = run_block(feats, nbrs[0], valid[0], conv_w[0], qkv_w[0], proj_weight[0])
    moved = jnp.zeros_like(first).at[hilbert_place].set(first)
    return run_block(moved, nbrs[1], valid[1], conv_w[1], qkv_w[1], proj_weight[1]).T
```

```python
import functools

import jax
import jax.numpy as jnp
from jax import lax
from jax.experimental import pallas as pl
from jax.experimental.pallas import tpu as pltpu
from jax.sharding import PartitionSpec as P

PATCH = 1024
HD = 16
REACH = 256
TAPS = 27
CAP = 16
MESH = pl.DeviceIdType.MESH
BF16 = jnp.bfloat16
F32 = jnp.float32


def remote(src, dst, send, recv, s, h):
    return pltpu.make_async_remote_copy(
        src_ref=src,
        dst_ref=dst,
        send_sem=send,
        recv_sem=recv,
        device_id=(s, h),
        device_id_type=MESH,
    )


def block_kernel(
    block,
    x,
    nbr,
    valid,
    cw,
    aw,
    pw,
    out,
    table,
    nb,
    vm,
    w,
    a,
    p,
    y,
    mix,
    kt,
    qm,
    va,
    ho,
    pt,
    local,
    s1,
    r1,
    s2,
    r2,
    s3,
    r3,
    s4,
    r4,
    s5,
    r5,
):
    width, rows = out.shape
    heads = width // HD
    groups = lax.axis_size("head")
    shards = lax.axis_size("seq")
    s = lax.axis_index("seq")
    h = lax.axis_index("head")
    after = lax.rem(s + 1, shards)
    before = lax.rem(s + shards - 1, shards)
    peers = [lax.rem(h + d, groups) for d in range(1, groups)]
    froms = [lax.rem(h + groups - d, groups) for d in range(1, groups)]
    blocks = rows // REACH

    def part(index, size=width, extra=0):
        return pl.ds(pl.multiple_of(index * width + extra, 16), size)

    mine = part(h)

    barrier = pltpu.get_barrier_semaphore()
    for other in peers:
        pl.semaphore_signal(barrier, inc=1, device_id=(s, other), device_id_type=MESH)
    for other in (before, after):
        pl.semaphore_signal(barrier, inc=1, device_id=(other, h), device_id_type=MESH)
    loads = [
        pltpu.make_async_copy(x, table.at[mine, pl.ds(REACH, rows)], local.at[0]),
        pltpu.make_async_copy(nbr.at[block], nb, local.at[1]),
        pltpu.make_async_copy(valid, vm, local.at[2]),
        pltpu.make_async_copy(cw.at[block], w, local.at[3]),
        pltpu.make_async_copy(aw.at[block], a, local.at[4]),
        pltpu.make_async_copy(pw.at[block], p.at[mine, :], local.at[5]),
    ]
    for load in loads:
        load.start()
    pl.semaphore_wait(barrier, groups + 1)

    pieces = ((0, REACH), (rows - REACH, REACH), (REACH, rows - 2 * REACH))
    sends = []
    for j, (low, size) in enumerate(pieces):
        for d, other in enumerate(peers):
            copy = remote(
                x.at[:, pl.ds(low, size)],
                table.at[mine, pl.ds(REACH + low, size)],
                s1.at[j, d],
                r1.at[j, d],
                s,
                other,
            )
            copy.start()
            sends.append(copy)

    def arrived(j):
        low, size = pieces[j]
        for d, other in enumerate(froms):
            remote(
                x.at[:, pl.ds(low, size)],
                table.at[part(other), pl.ds(REACH + low, size)],
                s1.at[j, d],
                r1.at[j, d],
                s,
                other,
            ).wait_recv()

    loads[0].wait()
    arrived(0)
    first = remote(
        table.at[:, pl.ds(REACH, REACH)],
        table.at[:, pl.ds(REACH + rows, REACH)],
        s2.at[0],
        r2.at[0],
        before,
        h,
    )
    first.start()
    arrived(1)
    last = remote(
        table.at[:, pl.ds(rows, REACH)],
        table.at[:, pl.ds(0, REACH)],
        s2.at[1],
        r2.at[1],
        after,
        h,
    )
    last.start()
    sends += [first, last]
    loads[5].wait()
    for d, other in enumerate(peers):
        copy = remote(p.at[mine, :], p.at[mine, :], s5.at[d], r5.at[d], s, other)
        copy.start()
        sends.append(copy)
    for load in loads[1:5]:
        load.wait()
    arrived(2)

    step = 9

    def products(tile):
        points = table[:, tile * REACH : (tile + 1) * REACH]

        def some(i, carry):
            taps = w[pl.ds(i * step, step)].reshape(step * width, -1)
            value = jnp.dot(taps, points, preferred_element_type=F32).astype(BF16)
            y[pl.ds(i * step, step), tile] = value.reshape(step, width, REACH)
            return carry

        lax.fori_loop(0, TAPS // step, some, 0)

    for tile in range(1, blocks + 1):
        products(tile)
    first.wait_recv()
    last.wait_recv()
    products(0)
    products(blocks + 1)

    place = lax.broadcasted_iota(jnp.int32, (REACH, REACH), 0)
    for blk in range(blocks):
        cols = slice(blk * REACH, (blk + 1) * REACH)
        base = s * rows + (blk - 1) * REACH

        def tap(t, total):
            index = nb[pl.ds(t, 1), cols]
            spot = index - base
            tile = jnp.where(index < 0, 3, spot >> 8)
            pick = (place == (spot & (REACH - 1))).astype(F32).astype(BF16)
            terms = y[t, blk : blk + 3].reshape(3 * width, REACH)
            picked = jnp.dot(terms, pick, preferred_element_type=F32)
            term = jnp.where(tile == 0, picked[:width], 0.0)
            term = jnp.where(tile == 1, picked[width : 2 * width], term)
            term = jnp.where(tile == 2, picked[2 * width :], term)
            return total + term

        total = lax.fori_loop(0, TAPS, tap, jnp.zeros((width, REACH), F32), unroll=3)
        own = table[mine, REACH + blk * REACH : REACH + (blk + 1) * REACH].astype(F32)
        mix[mine, cols] = (own + total).astype(BF16)
        for d, other in enumerate(peers):
            copy = remote(mix.at[mine, cols], mix.at[mine, cols], s3.at[blk, d], r3.at[blk, d], s, other)
            copy.start()
            sends.append(copy)

    scale = 1.0 / HD**0.5
    bias = jnp.where(vm[block : block + 1, :] > 0, 0.0, -1e30)
    ones = jnp.where(lax.broadcasted_iota(jnp.int32, (HD, rows), 0) == 0, 1.0, 0.0).astype(BF16)
    qm[...] = jnp.zeros(qm.shape, BF16)
    for hd in range(heads):
        qm[hd, width : width + HD, :] = ones
        va[hd, HD:, :] = ones
    weights = a[...].reshape(3 * width, -1)
    for blk in range(blocks):
        cols = slice(blk * REACH, (blk + 1) * REACH)
        for d, other in enumerate(froms):
            theirs = mix.at[part(other), cols]
            remote(theirs, theirs, s3.at[blk, d], r3.at[blk, d], s, other).wait_recv()
        values = mix[:, cols].astype(F32)
        centred = values - jnp.mean(values, axis=0, keepdims=True)
        spread = jnp.mean(centred * centred, axis=0, keepdims=True)
        normed = (centred * lax.rsqrt(spread + 1e-05)).astype(BF16)
        qkv = jnp.dot(weights, normed, preferred_element_type=F32)
        query = (qkv[:width].astype(BF16).astype(F32) * scale).astype(BF16)
        value = qkv[2 * width :].astype(BF16)
        for hd in range(heads):
            span = slice(hd * HD, (hd + 1) * HD)
            qm[hd, span, cols] = query[span]
            va[hd, :HD, cols] = value[span]
        tail = jnp.where(
            lax.broadcasted_iota(jnp.int32, (width, REACH), 0) == 0, bias[:, cols], 0.0
        )
        keys = jnp.concatenate([qkv[width : 2 * width], tail], axis=0)
        kt[cols, :] = keys.T.astype(BF16)

    for d, other in enumerate(froms):
        theirs = p.at[part(other), :]
        remote(theirs, theirs, s5.at[d], r5.at[d], s, other).wait_recv()
    pt[...] = p[...].astype(F32).T.astype(BF16)

    for hd in range(heads):
        for blk in range(blocks):
            cols = slice(blk * REACH, (blk + 1) * REACH)
            scores = jnp.dot(kt[...], qm[hd, :, cols], preferred_element_type=F32)
            top = jnp.max(scores, axis=0, keepdims=True)
            probs = jnp.exp(scores - top).astype(BF16)
            summed = jnp.dot(va[hd], probs, preferred_element_type=F32)
            result = summed[:HD] / summed[HD : HD + 1]
            ho[part(h, HD, hd * HD), cols] = result.astype(BF16)
        span = part(h, HD, hd * HD)
        for d, other in enumerate(peers):
            copy = remote(ho.at[span, :], ho.at[span, :], s4.at[hd, d], r4.at[hd, d], s, other)
            copy.start()
            sends.append(copy)
    for hd in range(heads):
        for d, other in enumerate(froms):
            theirs = ho.at[part(other, HD, hd * HD), :]
            remote(theirs, theirs, s4.at[hd, d], r4.at[hd, d], s, other).wait_recv()
    update = jnp.dot(pt[mine, :], ho[...], preferred_element_type=F32)
    out[...] = (mix[mine, :].astype(F32) + update).astype(BF16)
    for copy in sends:
        copy.wait_send()


def run_block(block, groups, x, nbr, valid, cw, aw, pw):
    width, rows = x.shape
    channels = width * groups
    heads = width // HD
    blocks = rows // REACH
    others = groups - 1
    dma = pltpu.SemaphoreType.DMA
    return pl.pallas_call(
        functools.partial(block_kernel, block),
        out_shape=jax.ShapeDtypeStruct((width, rows), BF16),
        in_specs=[pl.BlockSpec(memory_space=pl.ANY)] * 6,
        out_specs=pl.BlockSpec(memory_space=pltpu.VMEM),
        scratch_shapes=[
            pltpu.VMEM((channels, rows + 2 * REACH), BF16),
            pltpu.VMEM((TAPS, rows), jnp.int32),
            pltpu.VMEM((2, rows), jnp.int32),
            pltpu.VMEM((TAPS, width, channels), BF16),
            pltpu.VMEM((3, width, channels), BF16),
            pltpu.VMEM((channels, channels), BF16),
            pltpu.VMEM((TAPS, blocks + 2, width, REACH), BF16),
            pltpu.VMEM((channels, rows), BF16),
            pltpu.VMEM((rows, 2 * width), BF16),
            pltpu.VMEM((heads, 2 * width, rows), BF16),
            pltpu.VMEM((heads, 2 * HD, rows), BF16),
            pltpu.VMEM((channels, rows), BF16),
            pltpu.VMEM((channels, channels), BF16),
            dma((6,)),
            dma((3, others)),
            dma((3, others)),
            dma((2,)),
            dma((2,)),
            dma((blocks, others)),
            dma((blocks, others)),
            dma((heads, others)),
            dma((heads, others)),
            dma((others,)),
            dma((others,)),
        ],
        compiler_params=pltpu.CompilerParams(
            collective_id=block, has_side_effects=True, vmem_limit_bytes=48 * 2**20
        ),
        name=f"block{block}",
    )(x, nbr, valid, cw, aw, pw)


def order_kernel(x, places, out, pv, feats, tri, pick, going, come, land, flat, turned, local, s1, r1, s2, r2):
    width, rows = x.shape
    chips = places.shape[0]
    lines = places.shape[1]
    lanes = places.shape[2]
    s = lax.axis_index("seq")
    h = lax.axis_index("head")
    core = lax.rem(s, 2)
    chip = s // 2
    sibling = s + 1 - 2 * core

    barrier = pltpu.get_barrier_semaphore()

    def greet(i, carry):
        other = lax.rem(chip + i, chips) * 2 + core
        pl.semaphore_signal(barrier, inc=1, device_id=(other, h), device_id_type=MESH)
        return carry

    pl.semaphore_signal(barrier, inc=1, device_id=(sibling, h), device_id_type=MESH)
    lax.fori_loop(1, chips, greet, 0)
    load = pltpu.make_async_copy(places, pv, local.at[0])
    load.start()
    keep = pltpu.make_async_copy(x, feats.at[core], local.at[1])
    keep.start()
    load.wait()
    pl.semaphore_wait(barrier, chips)
    swap = remote(x, feats.at[core], s1.at[0], r1.at[0], sibling, h)
    swap.start()

    low = lax.broadcasted_iota(jnp.int32, (lanes, lanes), 0)
    high = lax.broadcasted_iota(jnp.int32, (lanes, lanes), 1)
    tri[...] = jnp.where(low <= high, 1.0, 0.0).astype(BF16)

    column = lax.broadcasted_iota(jnp.int32, (chips, lanes), 0)
    run = jnp.zeros((chips, 1), F32)
    slots = []
    for line in range(lines):
        row = pv[chip, line : line + 1, :]
        device = row // rows
        mask = jnp.where(device == column * 2 + core, 1.0, 0.0)
        counts = jnp.dot(mask.astype(BF16), tri[...], preferred_element_type=F32) + run
        run = counts[:, lanes - 1 :]
        rank = (jnp.sum(mask * counts, axis=0, keepdims=True) - 1.0).astype(jnp.int32)
        here = lax.rem(device, 2) == core
        target = (device // 2) * CAP + (rank & (CAP - 1))
        slots.append((jnp.where(here, target, -1), rank // CAP))
    targets = jnp.concatenate([t for t, _ in slots], axis=1)
    halves = jnp.concatenate([e for _, e in slots], axis=1)
    for e in range(2):
        pick[e : e + 1, :] = jnp.where(halves == e, targets, -1)

    keep.wait()
    swap.wait_recv()
    points = jnp.concatenate([feats[0], feats[1]], axis=1)
    strip = 16 * CAP
    strips = chips // 16
    own = chip // 16
    spot = lax.broadcasted_iota(jnp.int32, (strip, 2 * rows), 0)
    nt = (((1,), (1,)), ((), ()))

    def sort(i, carry):
        which = lax.rem(own + i, strips)
        sides = []
        for e in range(2):
            onehot = (spot + which * strip == pick[e : e + 1, :]).astype(F32).astype(BF16)
            sides.append(lax.dot_general(onehot, points, nt, preferred_element_type=F32))
        both = jnp.concatenate(sides, axis=1).astype(BF16)
        going[pl.ds(which * 16, 16)] = both.reshape(16, CAP, 2 * width)

        def send(j, c):
            other = which * 16 + lax.rem(chip + j, 16)

            @pl.when(other != chip)
            def _():
                remote(going.at[other], come.at[chip], s2.at[0], r2.at[0], other * 2 + core, h).start()

            return c

        lax.fori_loop(0, 16, send, 0)
        return carry

    lax.fori_loop(0, strips, sort, 0)
    stay = pltpu.make_async_copy(going.at[chip], come.at[chip], local.at[2])
    stay.start()

    run = jnp.zeros((chips, 1), F32)
    for line in range(lines):
        row = pv[:, line, :]
        mask = jnp.where(row // rows == s, 1.0, 0.0)
        counts = jnp.dot(mask.astype(BF16), tri[...], preferred_element_type=F32) + run
        run = counts[:, lanes - 1 :]
        land[line] = jnp.where(mask > 0, counts - 1.0, -1.0)
        flat[line] = ((row & (rows - 1)) + 1).astype(F32)
    where = lax.broadcasted_iota(jnp.int32, (chips, rows), 1).astype(F32) + 1.0

    def settle(k, carry):
        found = jnp.zeros((chips, lanes), F32)
        for line in range(lines):
            found += jnp.where(land[line] == k.astype(F32), flat[line], 0.0)
        spots = jnp.sum(found, axis=1, keepdims=True)
        turned[pl.ds(pl.multiple_of(k * chips, 16), chips), :] = (spots == where).astype(F32).astype(BF16)
        return carry

    lax.fori_loop(0, 2 * CAP, settle, 0)

    stay.wait()
    many = pl.ds(0, chips - 1)
    every = remote(going.at[many], come.at[many], s2.at[0], r2.at[0], sibling, h)
    every.wait_recv()
    arrived = come[...].astype(F32)
    parts = []
    for k in range(0, CAP, 2):
        two = jnp.concatenate([arrived[:, k, :], arrived[:, k + 1, :]], axis=0)
        parts.append(two.T.astype(BF16))
    packed = jnp.concatenate(parts, axis=1)
    half = CAP * chips
    total = jnp.dot(packed[:width], turned[:half, :], preferred_element_type=F32)
    total += jnp.dot(packed[width:], turned[half:, :], preferred_element_type=F32)
    out[...] = total.astype(BF16)
    swap.wait_send()
    every.wait_send()


def change_order(x, places):
    width, rows = x.shape
    chips, lines, lanes = places.shape
    dma = pltpu.SemaphoreType.DMA
    return pl.pallas_call(
        order_kernel,
        out_shape=jax.ShapeDtypeStruct((width, rows), BF16),
        in_specs=[pl.BlockSpec(memory_space=pl.ANY)] * 2,
        out_specs=pl.BlockSpec(memory_space=pltpu.VMEM),
        scratch_shapes=[
            pltpu.VMEM((chips, lines, lanes), jnp.int32),
            pltpu.VMEM((2, width, rows), BF16),
            pltpu.VMEM((lanes, lanes), BF16),
            pltpu.VMEM((2, 2 * rows), jnp.int32),
            pltpu.VMEM((chips, CAP, 2 * width), BF16),
            pltpu.VMEM((chips, CAP, 2 * width), BF16),
            pltpu.VMEM((lines, chips, lanes), F32),
            pltpu.VMEM((lines, chips, lanes), F32),
            pltpu.VMEM((2 * CAP * chips, rows), BF16),
            dma((3,)),
            dma((1,)),
            dma((1,)),
            dma((1,)),
            dma((1,)),
        ],
        compiler_params=pltpu.CompilerParams(
            collective_id=2, has_side_effects=True, vmem_limit_bytes=48 * 2**20
        ),
        name="change_order",
    )(x, places)


def body(groups, features, neighbours, valid, conv_weight, attn_weight, proj_weight, hilbert_place):
    rows = hilbert_place.shape[0]
    places = lax.all_gather(hilbert_place.reshape(1, rows // 128, 128), "seq", axis=0, tiled=True)
    shards = places.shape[0]
    places = places.reshape(shards // 2, rows // 64, 128)
    rest = (neighbours, valid, conv_weight, attn_weight, proj_weight)
    first = run_block(0, groups, features, *rest)
    moved = change_order(first, places)
    return run_block(1, groups, moved, *rest)


def solution(mesh):
    in_specs = (
        P("head", "seq"),
        P(None, None, "seq"),
        P(None, "seq"),
        P(None, None, "head", None),
        P(None, None, "head", None),
        P(None, "head", None),
        P("seq"),
    )
    out_specs = P("head", "seq")
    return jax.shard_map(
        functools.partial(body, mesh.shape["head"]),
        mesh=mesh,
        in_specs=in_specs,
        out_specs=out_specs,
        check_vma=False,
    )
```

```python
import functools
import math

import jax
import jax.numpy as jnp
from jax import lax
from jax.experimental import pallas as pl
from jax.experimental.pallas import tpu as pltpu
from jax.sharding import PartitionSpec as P

PATCH = 1024
HD = 16
REACH = 256
TAPS = 27
CAP = 16
MESH = pl.DeviceIdType.MESH
BF16 = jnp.bfloat16
F32 = jnp.float32


def remote(src, dst, send, recv, s, h):
    return pltpu.make_async_remote_copy(
        src_ref=src,
        dst_ref=dst,
        send_sem=send,
        recv_sem=recv,
        device_id=(s, h),
        device_id_type=MESH,
    )


def block_kernel(block, x, nbr, valid, cw, aw, pw, *rest):
    if block == 0:
        place, out, places, *rest = rest
        *rest, s6, r6, s7, r7, s8, r8 = rest
    else:
        out, *rest = rest
    block_steps(block, x, nbr, valid, cw, aw, pw, out, *rest, (place, places, s6, r6, s7, r7, s8, r8) if block == 0 else None)


def block_steps(
    block,
    x,
    nbr,
    valid,
    cw,
    aw,
    pw,
    out,
    table,
    nb,
    vm,
    w,
    a,
    p,
    y,
    mix,
    kt,
    qm,
    va,
    ho,
    pt,
    local,
    s1,
    r1,
    s2,
    r2,
    s3,
    r3,
    s4,
    r4,
    s5,
    r5,
    spread_places,
):
    width, rows = out.shape
    heads = width // HD
    groups = lax.axis_size("head")
    shards = lax.axis_size("seq")
    s = lax.axis_index("seq")
    h = lax.axis_index("head")
    after = lax.rem(s + 1, shards)
    before = lax.rem(s + shards - 1, shards)
    peers = [lax.rem(h + d, groups) for d in range(1, groups)]
    froms = [lax.rem(h + groups - d, groups) for d in range(1, groups)]
    blocks = rows // REACH

    def part(index, size=width, extra=0):
        return pl.ds(pl.multiple_of(index * width + extra, 16), size)

    mine = part(h)

    barrier = pltpu.get_barrier_semaphore()
    for other in peers:
        pl.semaphore_signal(barrier, inc=1, device_id=(s, other), device_id_type=MESH)
    for other in (before, after):
        pl.semaphore_signal(barrier, inc=1, device_id=(other, h), device_id_type=MESH)
    greeted = groups + 1
    if spread_places is not None:
        place, places, s6, r6, s7, r7, s8, r8 = spread_places
        side = places.shape[0]
        core = lax.rem(s, 2)
        zz = s // (2 * side)
        yy = lax.rem(s // 2, side)
        sibling = s + 1 - 2 * core
        lines = [lax.rem(zz + d, side) for d in range(1, side)]
        ranks = [lax.rem(yy + d, side) for d in range(1, side)]
        for other in [(q * side + yy) * 2 + core for q in lines] + [(zz * side + q) * 2 + core for q in ranks]:
            pl.semaphore_signal(barrier, inc=1, device_id=(other, h), device_id_type=MESH)
        greeted += 2 * (side - 1)
    loads = [
        pltpu.make_async_copy(x, table.at[mine, pl.ds(REACH, rows)], local.at[0]),
        pltpu.make_async_copy(nbr, nb, local.at[1]),
        pltpu.make_async_copy(valid, vm, local.at[2]),
        pltpu.make_async_copy(cw.at[block], w, local.at[3]),
        pltpu.make_async_copy(aw.at[block], a, local.at[4]),
        pltpu.make_async_copy(pw.at[block], p.at[mine, :], local.at[5]),
    ]
    if spread_places is not None:
        loads.append(pltpu.make_async_copy(place, places.at[zz, yy, core], local.at[6]))
    for load in loads:
        load.start()
    pl.semaphore_wait(barrier, greeted)

    pieces = ((0, REACH), (rows - REACH, REACH), (REACH, rows - 2 * REACH))
    sends = []
    for j, (low, size) in enumerate(pieces):
        for d, other in enumerate(peers):
            copy = remote(
                x.at[:, pl.ds(low, size)],
                table.at[mine, pl.ds(REACH + low, size)],
                s1.at[j, d],
                r1.at[j, d],
                s,
                other,
            )
            copy.start()
            sends.append(copy)

    if spread_places is not None:
        for d, other in enumerate(lines):
            copy = remote(place, places.at[zz, yy, core], s6.at[d], r6.at[d], (other * side + yy) * 2 + core, h)
            copy.start()
            sends.append(copy)

    def arrived(j):
        low, size = pieces[j]
        for d, other in enumerate(froms):
            remote(
                x.at[:, pl.ds(low, size)],
                table.at[part(other), pl.ds(REACH + low, size)],
                s1.at[j, d],
                r1.at[j, d],
                s,
                other,
            ).wait_recv()

    loads[0].wait()
    arrived(0)
    first = remote(
        table.at[:, pl.ds(REACH, REACH)],
        table.at[:, pl.ds(REACH + rows, REACH)],
        s2.at[0],
        r2.at[0],
        before,
        h,
    )
    first.start()
    arrived(1)
    last = remote(
        table.at[:, pl.ds(rows, REACH)],
        table.at[:, pl.ds(0, REACH)],
        s2.at[1],
        r2.at[1],
        after,
        h,
    )
    last.start()
    sends += [first, last]
    loads[5].wait()
    for d, other in enumerate(peers):
        copy = remote(p.at[mine, :], p.at[mine, :], s5.at[d], r5.at[d], s, other)
        copy.start()
        sends.append(copy)
    for load in loads[1:5]:
        load.wait()
    arrived(2)
    if spread_places is not None:
        loads[6].wait()
        for d in range(1, side):
            theirs = places.at[lax.rem(zz + side - d, side), yy, core]
            remote(place, theirs, s6.at[d - 1], r6.at[d - 1], s, h).wait_recv()
        for d, other in enumerate(ranks):
            column = places.at[:, yy, core]
            copy = remote(column, column, s7.at[d], r7.at[d], (zz * side + other) * 2 + core, h)
            copy.start()
            sends.append(copy)

    taps = w[...].reshape(TAPS * width, -1)

    def products(tile):
        points = table[:, tile * REACH : (tile + 1) * REACH]
        value = jnp.dot(taps, points, preferred_element_type=F32).astype(BF16)
        y[:, tile] = value.reshape(TAPS, width, REACH)

    for tile in range(1, blocks + 1):
        products(tile)
    if spread_places is not None:
        for d in range(1, side):
            theirs = places.at[:, lax.rem(yy + side - d, side), core]
            remote(theirs, theirs, s7.at[d - 1], r7.at[d - 1], s, h).wait_recv()
        column = places.at[:, :, core]
        across = remote(column, column, s8.at[0], r8.at[0], sibling, h)
        across.start()
        sends.append(across)
    first.wait_recv()
    last.wait_recv()
    products(0)
    products(blocks + 1)

    position = lax.broadcasted_iota(jnp.int32, (REACH, REACH), 0).astype(F32).astype(BF16)
    one, zero = jnp.ones((), BF16), jnp.zeros((), BF16)
    for blk in range(blocks):
        cols = slice(blk * REACH, (blk + 1) * REACH)
        base = s * rows + (blk - 1) * REACH
        total = jnp.zeros((width, REACH), F32)
        for t in range(TAPS):
            index = nb[t, block : block + 1, cols]
            spot = index - base
            tile = jnp.where(index < 0, 3, spot >> 8)
            within = (spot & (REACH - 1)).astype(F32).astype(BF16)
            pick = jnp.where(position == within, one, zero)
            terms = y[t, blk : blk + 3].reshape(3 * width, REACH)
            picked = jnp.dot(terms, pick, preferred_element_type=F32)
            term = jnp.where(tile == 0, picked[:width], 0.0)
            term = jnp.where(tile == 1, picked[width : 2 * width], term)
            term = jnp.where(tile == 2, picked[2 * width :], term)
            total = total + term
        own = table[mine, REACH + blk * REACH : REACH + (blk + 1) * REACH].astype(F32)
        mix[mine, cols] = (own + total).astype(BF16)
        for d, other in enumerate(peers):
            copy = remote(mix.at[mine, cols], mix.at[mine, cols], s3.at[blk, d], r3.at[blk, d], s, other)
            copy.start()
            sends.append(copy)

    scale = 1.0 / HD**0.5
    bias = jnp.where(vm[block : block + 1, :] > 0, 0.0, -1e30)
    ones = jnp.where(lax.broadcasted_iota(jnp.int32, (HD, rows), 0) == 0, 1.0, 0.0).astype(BF16)
    qm[...] = jnp.zeros(qm.shape, BF16)
    for hd in range(heads):
        qm[hd, width : width + HD, :] = ones
        va[hd, HD:, :] = ones
    weights = a[...].reshape(3 * width, -1)
    for blk in range(blocks):
        cols = slice(blk * REACH, (blk + 1) * REACH)
        for d, other in enumerate(froms):
            theirs = mix.at[part(other), cols]
            remote(theirs, theirs, s3.at[blk, d], r3.at[blk, d], s, other).wait_recv()
        values = mix[:, cols].astype(F32)
        centred = values - jnp.mean(values, axis=0, keepdims=True)
        spread = jnp.mean(centred * centred, axis=0, keepdims=True)
        normed = (centred * lax.rsqrt(spread + 1e-05)).astype(BF16)
        qkv = jnp.dot(weights, normed, preferred_element_type=F32)
        query = (qkv[:width].astype(BF16).astype(F32) * scale).astype(BF16)
        value = qkv[2 * width :].astype(BF16)
        for hd in range(heads):
            span = slice(hd * HD, (hd + 1) * HD)
            qm[hd, span, cols] = query[span]
            va[hd, :HD, cols] = value[span]
        tail = jnp.where(
            lax.broadcasted_iota(jnp.int32, (width, REACH), 0) == 0, bias[:, cols], 0.0
        )
        keys = jnp.concatenate([qkv[width : 2 * width], tail], axis=0)
        kt[cols, :] = keys.T.astype(BF16)

    for d, other in enumerate(froms):
        theirs = p.at[part(other), :]
        remote(theirs, theirs, s5.at[d], r5.at[d], s, other).wait_recv()
    pt[...] = p[...].astype(F32).T.astype(BF16)

    for hd in range(heads):
        scores = jnp.dot(kt[...], qm[hd], preferred_element_type=F32)
        top = jnp.max(scores, axis=0, keepdims=True)
        probs = jnp.exp((scores - top).astype(BF16))
        summed = jnp.dot(va[hd], probs, preferred_element_type=F32)
        result = summed[:HD] / summed[HD : HD + 1]
        ho[part(h, HD, hd * HD), :] = result.astype(BF16)
        span = part(h, HD, hd * HD)
        for d, other in enumerate(peers):
            copy = remote(ho.at[span, :], ho.at[span, :], s4.at[hd, d], r4.at[hd, d], s, other)
            copy.start()
            sends.append(copy)
    for hd in range(heads):
        for d, other in enumerate(froms):
            theirs = ho.at[part(other, HD, hd * HD), :]
            remote(theirs, theirs, s4.at[hd, d], r4.at[hd, d], s, other).wait_recv()
    update = jnp.dot(pt[mine, :], ho[...], preferred_element_type=F32)
    out[...] = (mix[mine, :].astype(F32) + update).astype(BF16)
    if spread_places is not None:
        theirs = places.at[:, :, 1 - core]
        remote(theirs, theirs, s8.at[0], r8.at[0], sibling, h).wait_recv()
    for copy in sends:
        copy.wait_send()


def run_block(block, groups, x, nbr, valid, cw, aw, pw, place=None, side=None):
    width, rows = x.shape
    channels = width * groups
    heads = width // HD
    blocks = rows // REACH
    others = groups - 1
    dma = pltpu.SemaphoreType.DMA
    given = [x, nbr, valid, cw, aw, pw]
    shapes = [jax.ShapeDtypeStruct((width, rows), BF16)]
    specs = [pl.BlockSpec(memory_space=pltpu.VMEM)]
    more = []
    if place is not None:
        given.append(place)
        shapes.append(jax.ShapeDtypeStruct((side, side, 2) + place.shape, jnp.int32))
        specs.append(pl.BlockSpec(memory_space=pl.ANY))
        more = [dma((n,)) for n in (side - 1, side - 1, side - 1, side - 1, 1, 1)]
    return pl.pallas_call(
        functools.partial(block_kernel, block),
        out_shape=shapes,
        in_specs=[pl.BlockSpec(memory_space=pl.ANY)] * len(given),
        out_specs=specs,
        scratch_shapes=[
            pltpu.VMEM((channels, rows + 2 * REACH), BF16),
            pltpu.VMEM((TAPS, 2, rows), jnp.int32),
            pltpu.VMEM((2, rows), jnp.int32),
            pltpu.VMEM((TAPS, width, channels), BF16),
            pltpu.VMEM((3, width, channels), BF16),
            pltpu.VMEM((channels, channels), BF16),
            pltpu.VMEM((TAPS, blocks + 2, width, REACH), BF16),
            pltpu.VMEM((channels, rows), BF16),
            pltpu.VMEM((rows, 2 * width), BF16),
            pltpu.VMEM((heads, 2 * width, rows), BF16),
            pltpu.VMEM((heads, 2 * HD, rows), BF16),
            pltpu.VMEM((channels, rows), BF16),
            pltpu.VMEM((channels, channels), BF16),
            dma((7,)),
            dma((3, others)),
            dma((3, others)),
            dma((2,)),
            dma((2,)),
            dma((blocks, others)),
            dma((blocks, others)),
            dma((heads, others)),
            dma((heads, others)),
            dma((others,)),
            dma((others,)),
            *more,
        ],
        compiler_params=pltpu.CompilerParams(
            collective_id=block, has_side_effects=True, vmem_limit_bytes=60 * 2**20
        ),
        name=f"block{block}",
    )(*given)


def order_kernel(x, places, out, pv, feats, tri, pick, going, come, land, flat, turned, local, s1, r1, s2, r2):
    width, rows = x.shape
    chips = places.shape[0]
    lines = places.shape[1]
    lanes = places.shape[2]
    s = lax.axis_index("seq")
    h = lax.axis_index("head")
    core = lax.rem(s, 2)
    chip = s // 2
    sibling = s + 1 - 2 * core

    barrier = pltpu.get_barrier_semaphore()

    def greet(i, carry):
        other = lax.rem(chip + i, chips) * 2 + core
        pl.semaphore_signal(barrier, inc=1, device_id=(other, h), device_id_type=MESH)
        return carry

    pl.semaphore_signal(barrier, inc=1, device_id=(sibling, h), device_id_type=MESH)
    lax.fori_loop(1, chips, greet, 0)
    load = pltpu.make_async_copy(places, pv, local.at[0])
    load.start()
    keep = pltpu.make_async_copy(x, feats.at[core], local.at[1])
    keep.start()
    load.wait()
    pl.semaphore_wait(barrier, chips)
    swap = remote(x, feats.at[core], s1.at[0], r1.at[0], sibling, h)
    swap.start()

    low = lax.broadcasted_iota(jnp.int32, (lanes, lanes), 0)
    high = lax.broadcasted_iota(jnp.int32, (lanes, lanes), 1)
    tri[...] = jnp.where(low <= high, 1.0, 0.0).astype(BF16)

    column = lax.broadcasted_iota(jnp.int32, (chips, lanes), 0)
    run = jnp.zeros((chips, 1), F32)
    slots = []
    for line in range(lines):
        row = pv[chip, line : line + 1, :]
        device = row // rows
        mask = jnp.where(device == column * 2 + core, 1.0, 0.0)
        counts = jnp.dot(mask.astype(BF16), tri[...], preferred_element_type=F32) + run
        run = counts[:, lanes - 1 :]
        rank = (jnp.sum(mask * counts, axis=0, keepdims=True) - 1.0).astype(jnp.int32)
        here = lax.rem(device, 2) == core
        target = (device // 2) * CAP + (rank & (CAP - 1))
        slots.append((jnp.where(here, target, -1), rank // CAP))
    targets = jnp.concatenate([t for t, _ in slots], axis=1)
    halves = jnp.concatenate([e for _, e in slots], axis=1)
    for e in range(2):
        pick[e : e + 1, :] = jnp.where(halves == e, targets, -1)

    keep.wait()
    swap.wait_recv()
    points = jnp.concatenate([feats[0], feats[1]], axis=1)
    strip = 16 * CAP
    strips = chips // 16
    own = chip // 16
    spot = lax.broadcasted_iota(jnp.int32, (strip, 2 * rows), 0)
    nt = (((1,), (1,)), ((), ()))

    def sort(i, carry):
        which = lax.rem(own + i, strips)
        sides = []
        for e in range(2):
            onehot = (spot + which * strip == pick[e : e + 1, :]).astype(F32).astype(BF16)
            sides.append(lax.dot_general(onehot, points, nt, preferred_element_type=F32))
        both = jnp.concatenate(sides, axis=1).astype(BF16)
        going[pl.ds(which * 16, 16)] = both.reshape(16, CAP, 2 * width)

        def send(j, c):
            other = which * 16 + lax.rem(chip + j, 16)

            @pl.when(other != chip)
            def _():
                remote(going.at[other], come.at[chip], s2.at[0], r2.at[0], other * 2 + core, h).start()

            return c

        lax.fori_loop(0, 16, send, 0)
        return carry

    lax.fori_loop(0, strips, sort, 0)
    stay = pltpu.make_async_copy(going.at[chip], come.at[chip], local.at[2])
    stay.start()

    run = jnp.zeros((chips, 1), F32)
    for line in range(lines):
        row = pv[:, line, :]
        mask = jnp.where(row // rows == s, 1.0, 0.0)
        counts = jnp.dot(mask.astype(BF16), tri[...], preferred_element_type=F32) + run
        run = counts[:, lanes - 1 :]
        land[line] = jnp.where(mask > 0, counts - 1.0, -1.0)
        flat[line] = ((row & (rows - 1)) + 1).astype(F32)
    where = lax.broadcasted_iota(jnp.int32, (chips, rows), 1).astype(F32) + 1.0

    def settle(k, carry):
        found = jnp.zeros((chips, lanes), F32)
        for line in range(lines):
            found += jnp.where(land[line] == k.astype(F32), flat[line], 0.0)
        spots = jnp.sum(found, axis=1, keepdims=True)
        turned[pl.ds(pl.multiple_of(k * chips, 16), chips), :] = (spots == where).astype(F32).astype(BF16)
        return carry

    lax.fori_loop(0, 2 * CAP, settle, 0)

    stay.wait()
    many = pl.ds(0, chips - 1)
    every = remote(going.at[many], come.at[many], s2.at[0], r2.at[0], sibling, h)
    every.wait_recv()
    arrived = come[...].astype(F32)
    parts = []
    for k in range(0, CAP, 2):
        two = jnp.concatenate([arrived[:, k, :], arrived[:, k + 1, :]], axis=0)
        parts.append(two.T.astype(BF16))
    packed = jnp.concatenate(parts, axis=1)
    half = CAP * chips
    total = jnp.dot(packed[:width], turned[:half, :], preferred_element_type=F32)
    total += jnp.dot(packed[width:], turned[half:, :], preferred_element_type=F32)
    out[...] = total.astype(BF16)
    swap.wait_send()
    every.wait_send()


def change_order(x, places):
    width, rows = x.shape
    chips, lines, lanes = places.shape
    dma = pltpu.SemaphoreType.DMA
    return pl.pallas_call(
        order_kernel,
        out_shape=jax.ShapeDtypeStruct((width, rows), BF16),
        in_specs=[pl.BlockSpec(memory_space=pl.ANY)] * 2,
        out_specs=pl.BlockSpec(memory_space=pltpu.VMEM),
        scratch_shapes=[
            pltpu.VMEM((chips, lines, lanes), jnp.int32),
            pltpu.VMEM((2, width, rows), BF16),
            pltpu.VMEM((lanes, lanes), BF16),
            pltpu.VMEM((2, 2 * rows), jnp.int32),
            pltpu.VMEM((chips, CAP, 2 * width), BF16),
            pltpu.VMEM((chips, CAP, 2 * width), BF16),
            pltpu.VMEM((lines, chips, lanes), F32),
            pltpu.VMEM((lines, chips, lanes), F32),
            pltpu.VMEM((2 * CAP * chips, rows), BF16),
            dma((3,)),
            dma((1,)),
            dma((1,)),
            dma((1,)),
            dma((1,)),
        ],
        compiler_params=pltpu.CompilerParams(
            collective_id=2, has_side_effects=True, vmem_limit_bytes=60 * 2**20
        ),
        name="change_order",
    )(x, places)


def body(groups, side, features, neighbours, valid, conv_weight, attn_weight, proj_weight, hilbert_place):
    rows = hilbert_place.shape[0]
    rest = (jnp.swapaxes(neighbours, 0, 1), valid, conv_weight, attn_weight, proj_weight)
    first, places = run_block(0, groups, features, *rest, hilbert_place.reshape(rows // 128, 128), side)
    moved = change_order(first, places.reshape(side * side, rows // 64, 128))
    return run_block(1, groups, moved, *rest)[0]


def solution(mesh):
    in_specs = (
        P("head", "seq"),
        P(None, None, "seq"),
        P(None, "seq"),
        P(None, None, "head", None),
        P(None, None, "head", None),
        P(None, "head", None),
        P("seq"),
    )
    out_specs = P("head", "seq")
    return jax.shard_map(
        functools.partial(body, mesh.shape["head"], math.isqrt(mesh.shape["seq"] // 2)),
        mesh=mesh,
        in_specs=in_specs,
        out_specs=out_specs,
        check_vma=False,
    )
```

```python
import functools
import math

import jax
import jax.numpy as jnp
from jax import lax
from jax.experimental import pallas as pl
from jax.experimental.pallas import tpu as pltpu
from jax.sharding import PartitionSpec as P

PATCH = 1024
HD = 16
REACH = 256
TAPS = 27
CAP = 16
MESH = pl.DeviceIdType.MESH
BF16 = jnp.bfloat16
F32 = jnp.float32


def remote(src, dst, send, recv, s, h):
    return pltpu.make_async_remote_copy(
        src_ref=src,
        dst_ref=dst,
        send_sem=send,
        recv_sem=recv,
        device_id=(s, h),
        device_id_type=MESH,
    )


def block_kernel(block, x, nbr, valid, cw, aw, pw, *rest):
    if block == 0:
        place, out, places, *rest = rest
        *rest, s6, r6, s7, r7, s8, r8 = rest
    else:
        out, *rest = rest
    block_steps(block, x, nbr, valid, cw, aw, pw, out, *rest, (place, places, s6, r6, s7, r7, s8, r8) if block == 0 else None)


def block_steps(
    block,
    x,
    nbr,
    valid,
    cw,
    aw,
    pw,
    out,
    table,
    nb,
    vm,
    w,
    a,
    p,
    y,
    mix,
    kt,
    qm,
    va,
    ho,
    pt,
    local,
    s1,
    r1,
    s2,
    r2,
    s3,
    r3,
    s4,
    r4,
    s5,
    r5,
    spread_places,
):
    width, rows = out.shape
    heads = width // HD
    groups = lax.axis_size("head")
    shards = lax.axis_size("seq")
    s = lax.axis_index("seq")
    h = lax.axis_index("head")
    after = lax.rem(s + 1, shards)
    before = lax.rem(s + shards - 1, shards)
    right = lax.rem(h + 1, groups)
    left = lax.rem(h + groups - 1, groups)
    far = lax.rem(h + 2, groups)
    blocks = rows // REACH

    def part(index, size=width, extra=0):
        return pl.ds(pl.multiple_of(index * width + extra, 16), size)

    mine = part(h)

    barrier = pltpu.get_barrier_semaphore()
    for other in (right, left):
        pl.semaphore_signal(barrier, inc=1, device_id=(s, other), device_id_type=MESH)
    for other in (before, after):
        pl.semaphore_signal(barrier, inc=1, device_id=(other, h), device_id_type=MESH)
    greeted = 4
    if spread_places is not None:
        place, places, s6, r6, s7, r7, s8, r8 = spread_places
        side = places.shape[0]
        core = lax.rem(s, 2)
        zz = s // (2 * side)
        yy = lax.rem(s // 2, side)
        sibling = s + 1 - 2 * core
        lines = [lax.rem(zz + d, side) for d in range(1, side)]
        ranks = [lax.rem(yy + d, side) for d in range(1, side)]
        for other in [(q * side + yy) * 2 + core for q in lines] + [(zz * side + q) * 2 + core for q in ranks]:
            pl.semaphore_signal(barrier, inc=1, device_id=(other, h), device_id_type=MESH)
        greeted += 2 * (side - 1)
    loads = [
        pltpu.make_async_copy(x, table.at[mine, pl.ds(REACH, rows)], local.at[0]),
        pltpu.make_async_copy(nbr, nb, local.at[1]),
        pltpu.make_async_copy(valid, vm, local.at[2]),
        pltpu.make_async_copy(cw.at[block], w, local.at[3]),
        pltpu.make_async_copy(aw.at[block], a, local.at[4]),
        pltpu.make_async_copy(pw.at[block], p.at[mine, :], local.at[5]),
    ]
    if spread_places is not None:
        loads.append(pltpu.make_async_copy(place, places.at[zz, yy, core], local.at[6]))
    for load in loads:
        load.start()
    pl.semaphore_wait(barrier, greeted)

    sends = []

    def spread(source, piece, send, recv):
        for i, other in enumerate((right, left)):
            copy = remote(source, piece(h), send.at[i], recv.at[i], s, other)
            copy.start()
            sends.append(copy)

    def forward(piece, send, recv):
        for i, (origin, other) in enumerate(((left, right), (right, left))):
            theirs = piece(origin)
            remote(theirs, theirs, send.at[i], recv.at[i], s, other).wait_recv()
            half = piece(origin, i)
            copy = remote(half, half, send.at[2 + i], recv.at[2 + i], s, other)
            copy.start()
            sends.append(copy)

    def finish(piece, send, recv):
        for i in range(2):
            half = piece(far, i)
            remote(half, half, send.at[2 + i], recv.at[2 + i], s, right).wait_recv()

    def strip(ref, cols):
        def piece(index, half=None):
            if half is None:
                return ref.at[part(index), cols]
            return ref.at[part(index, width // 2, half * (width // 2)), cols]

        return piece

    pieces = ((0, REACH), (rows - REACH, REACH), (REACH, rows - 2 * REACH))
    inputs = [(strip(table, pl.ds(REACH + low, size)), s1.at[j], r1.at[j]) for j, (low, size) in enumerate(pieces)]
    for (low, size), item in zip(pieces, inputs):
        spread(x.at[:, pl.ds(low, size)], *item)
    if spread_places is not None:
        for d, other in enumerate(lines):
            copy = remote(place, places.at[zz, yy, core], s6.at[d], r6.at[d], (other * side + yy) * 2 + core, h)
            copy.start()
            sends.append(copy)

    loads[0].wait()
    forward(*inputs[0])
    forward(*inputs[1])
    finish(*inputs[0])
    first = remote(
        table.at[:, pl.ds(REACH, REACH)],
        table.at[:, pl.ds(REACH + rows, REACH)],
        s2.at[0],
        r2.at[0],
        before,
        h,
    )
    first.start()
    finish(*inputs[1])
    last = remote(
        table.at[:, pl.ds(rows, REACH)],
        table.at[:, pl.ds(0, REACH)],
        s2.at[1],
        r2.at[1],
        after,
        h,
    )
    last.start()
    sends += [first, last]
    for load in loads[1:5]:
        load.wait()

    taps = w[...].reshape(TAPS * width, -1)

    def products(tile):
        points = table[:, tile * REACH : (tile + 1) * REACH]
        value = jnp.dot(taps, points, preferred_element_type=F32).astype(BF16)
        y[:, tile] = value.reshape(TAPS, width, REACH)

    products(1)
    forward(*inputs[2])
    products(blocks)
    finish(*inputs[2])
    loads[5].wait()
    whole = (strip(p, pl.ds(0, p.shape[1])), s5, r5)
    spread(p.at[mine, :], *whole)
    for tile in range(2, blocks):
        products(tile)
    if spread_places is not None:
        loads[6].wait()
        for d in range(1, side):
            theirs = places.at[lax.rem(zz + side - d, side), yy, core]
            remote(place, theirs, s6.at[d - 1], r6.at[d - 1], s, h).wait_recv()
        for d, other in enumerate(ranks):
            column = places.at[:, yy, core]
            copy = remote(column, column, s7.at[d], r7.at[d], (zz * side + other) * 2 + core, h)
            copy.start()
            sends.append(copy)
    first.wait_recv()
    last.wait_recv()
    products(0)
    products(blocks + 1)

    position = lax.broadcasted_iota(jnp.int32, (REACH, REACH), 0).astype(F32).astype(BF16)
    one, zero = jnp.ones((), BF16), jnp.zeros((), BF16)
    mixes = [(strip(mix, pl.ds(blk * REACH, REACH)), s3.at[blk], r3.at[blk]) for blk in range(blocks)]
    for blk in range(blocks):
        cols = slice(blk * REACH, (blk + 1) * REACH)
        base = s * rows + (blk - 1) * REACH
        total = jnp.zeros((width, REACH), F32)
        for t in range(TAPS):
            index = nb[t, block : block + 1, cols]
            spot = index - base
            tile = jnp.where(index < 0, 3, spot >> 8)
            within = (spot & (REACH - 1)).astype(F32).astype(BF16)
            pick = jnp.where(position == within, one, zero)
            terms = y[t, blk : blk + 3].reshape(3 * width, REACH)
            picked = jnp.dot(terms, pick, preferred_element_type=F32)
            term = jnp.where(tile == 0, picked[:width], 0.0)
            term = jnp.where(tile == 1, picked[width : 2 * width], term)
            term = jnp.where(tile == 2, picked[2 * width :], term)
            total = total + term
        own = table[mine, REACH + blk * REACH : REACH + (blk + 1) * REACH].astype(F32)
        mix[mine, cols] = (own + total).astype(BF16)
        spread(mix.at[mine, cols], *mixes[blk])
        if blk >= 2:
            forward(*mixes[blk - 2])
    forward(*whole)
    if spread_places is not None:
        for d in range(1, side):
            theirs = places.at[:, lax.rem(yy + side - d, side), core]
            remote(theirs, theirs, s7.at[d - 1], r7.at[d - 1], s, h).wait_recv()
        column = places.at[:, :, core]
        across = remote(column, column, s8.at[0], r8.at[0], sibling, h)
        across.start()
        sends.append(across)

    scale = 1.0 / HD**0.5
    bias = jnp.where(vm[block : block + 1, :] > 0, 0.0, -1e30)
    ones = jnp.where(lax.broadcasted_iota(jnp.int32, (HD, rows), 0) == 0, 1.0, 0.0).astype(BF16)
    qm[...] = jnp.zeros(qm.shape, BF16)
    for hd in range(heads):
        qm[hd, width : width + HD, :] = ones
        va[hd, HD:, :] = ones
    weights = a[...].reshape(3 * width, -1)
    for blk in range(blocks):
        cols = slice(blk * REACH, (blk + 1) * REACH)
        if blk + blocks - 2 < blocks:
            forward(*mixes[blk + blocks - 2])
        finish(*mixes[blk])
        values = mix[:, cols].astype(F32)
        centred = values - jnp.mean(values, axis=0, keepdims=True)
        variance = jnp.mean(centred * centred, axis=0, keepdims=True)
        normed = (centred * lax.rsqrt(variance + 1e-05)).astype(BF16)
        qkv = jnp.dot(weights, normed, preferred_element_type=F32)
        query = (qkv[:width].astype(BF16).astype(F32) * scale).astype(BF16)
        value = qkv[2 * width :].astype(BF16)
        for hd in range(heads):
            span = slice(hd * HD, (hd + 1) * HD)
            qm[hd, span, cols] = query[span]
            va[hd, :HD, cols] = value[span]
        tail = jnp.where(
            lax.broadcasted_iota(jnp.int32, (width, REACH), 0) == 0, bias[:, cols], 0.0
        )
        keys = jnp.concatenate([qkv[width : 2 * width], tail], axis=0)
        kt[cols, :] = keys.T.astype(BF16)

    finish(*whole)
    pt[...] = p[...].astype(F32).T.astype(BF16)

    def lane(hd):
        def piece(index, half=None):
            cols = pl.ds(0, rows) if half is None else pl.ds(half * (rows // 2), rows // 2)
            return ho.at[part(index, HD, hd * HD), cols]

        return piece

    results = [(lane(hd), s4.at[hd], r4.at[hd]) for hd in range(heads)]
    for hd in range(heads):
        scores = jnp.dot(kt[...], qm[hd], preferred_element_type=F32)
        top = jnp.max(scores, axis=0, keepdims=True)
        probs = jnp.exp((scores - top).astype(BF16))
        summed = jnp.dot(va[hd], probs, preferred_element_type=F32)
        result = summed[:HD] / summed[HD : HD + 1]
        ho[part(h, HD, hd * HD), :] = result.astype(BF16)
        spread(ho.at[part(h, HD, hd * HD), :], *results[hd])
        if hd >= 1:
            forward(*results[hd - 1])
    forward(*results[heads - 1])
    for item in results:
        finish(*item)
    update = jnp.dot(pt[mine, :], ho[...], preferred_element_type=F32)
    out[...] = (mix[mine, :].astype(F32) + update).astype(BF16)
    if spread_places is not None:
        theirs = places.at[:, :, 1 - core]
        remote(theirs, theirs, s8.at[0], r8.at[0], sibling, h).wait_recv()
    for copy in sends:
        copy.wait_send()


def run_block(block, groups, x, nbr, valid, cw, aw, pw, place=None, side=None):
    width, rows = x.shape
    channels = width * groups
    heads = width // HD
    blocks = rows // REACH
    dma = pltpu.SemaphoreType.DMA
    given = [x, nbr, valid, cw, aw, pw]
    shapes = [jax.ShapeDtypeStruct((width, rows), BF16)]
    specs = [pl.BlockSpec(memory_space=pltpu.VMEM)]
    more = []
    if place is not None:
        given.append(place)
        shapes.append(jax.ShapeDtypeStruct((side, side, 2) + place.shape, jnp.int32))
        specs.append(pl.BlockSpec(memory_space=pl.ANY))
        more = [dma((n,)) for n in (side - 1, side - 1, side - 1, side - 1, 1, 1)]
    return pl.pallas_call(
        functools.partial(block_kernel, block),
        out_shape=shapes,
        in_specs=[pl.BlockSpec(memory_space=pl.ANY)] * len(given),
        out_specs=specs,
        scratch_shapes=[
            pltpu.VMEM((channels, rows + 2 * REACH), BF16),
            pltpu.VMEM((TAPS, 2, rows), jnp.int32),
            pltpu.VMEM((2, rows), jnp.int32),
            pltpu.VMEM((TAPS, width, channels), BF16),
            pltpu.VMEM((3, width, channels), BF16),
            pltpu.VMEM((channels, channels), BF16),
            pltpu.VMEM((TAPS, blocks + 2, width, REACH), BF16),
            pltpu.VMEM((channels, rows), BF16),
            pltpu.VMEM((rows, 2 * width), BF16),
            pltpu.VMEM((heads, 2 * width, rows), BF16),
            pltpu.VMEM((heads, 2 * HD, rows), BF16),
            pltpu.VMEM((channels, rows), BF16),
            pltpu.VMEM((channels, channels), BF16),
            dma((7,)),
            dma((3, 4)),
            dma((3, 4)),
            dma((2,)),
            dma((2,)),
            dma((blocks, 4)),
            dma((blocks, 4)),
            dma((heads, 4)),
            dma((heads, 4)),
            dma((4,)),
            dma((4,)),
            *more,
        ],
        compiler_params=pltpu.CompilerParams(
            collective_id=block, has_side_effects=True, vmem_limit_bytes=60 * 2**20
        ),
        name=f"block{block}",
    )(*given)


def order_kernel(x, places, out, pv, pl_own, feats, tri, pick, going, come, land, flat, found, turned, local, s1, r1, s2, r2):
    width, rows = x.shape
    chips = places.shape[0]
    lines = places.shape[1]
    lanes = places.shape[2]
    s = lax.axis_index("seq")
    h = lax.axis_index("head")
    core = lax.rem(s, 2)
    chip = s // 2
    sibling = s + 1 - 2 * core
    bits = rows.bit_length() - 1

    barrier = pltpu.get_barrier_semaphore()

    def greet(i, carry):
        other = lax.rem(chip + i, chips) * 2 + core
        pl.semaphore_signal(barrier, inc=1, device_id=(other, h), device_id_type=MESH)
        return carry

    pl.semaphore_signal(barrier, inc=1, device_id=(sibling, h), device_id_type=MESH)
    lax.fori_loop(1, chips, greet, 0)
    near = pltpu.make_async_copy(places.at[chip], pl_own, local.at[0])
    near.start()
    for line in range(lines):
        pltpu.make_async_copy(places.at[:, line], pv.at[line], local.at[3]).start()
    keep = pltpu.make_async_copy(x, feats.at[core], local.at[1])
    keep.start()
    near.wait()
    pl.semaphore_wait(barrier, chips)
    swap = remote(x, feats.at[core], s1.at[0], r1.at[0], sibling, h)
    swap.start()

    low = lax.broadcasted_iota(jnp.int32, (lanes, lanes), 0)
    high = lax.broadcasted_iota(jnp.int32, (lanes, lanes), 1)
    tri[...] = jnp.where(low <= high, 1.0, 0.0).astype(BF16)

    column = lax.broadcasted_iota(jnp.int32, (chips, lanes), 0)
    run = jnp.zeros((chips, 1), F32)
    slots = []
    for line in range(lines):
        row = pl_own[line : line + 1, :]
        device = row >> bits
        mask = jnp.where(device == column * 2 + core, 1.0, 0.0)
        counts = jnp.dot(mask.astype(BF16), tri[...], preferred_element_type=F32) + run
        run = counts[:, lanes - 1 :]
        rank = (jnp.sum(mask * counts, axis=0, keepdims=True) - 1.0).astype(jnp.int32)
        here = (device & 1) == core
        target = (device >> 1) * CAP + (rank & (CAP - 1))
        slots.append((jnp.where(here, target, -1), rank >> 4))
    targets = jnp.concatenate([t for t, _ in slots], axis=1)
    halves = jnp.concatenate([e for _, e in slots], axis=1)
    for e in range(2):
        pick[e : e + 1, :] = jnp.where(halves == e, targets, -1)

    keep.wait()
    swap.wait_recv()
    points = jnp.concatenate([feats[0], feats[1]], axis=1)
    strip = 16 * CAP
    strips = chips // 16
    own = chip // 16
    spot = lax.broadcasted_iota(jnp.int32, (strip, 2 * rows), 0)
    nt = (((1,), (1,)), ((), ()))

    def sort(i, carry):
        which = lax.rem(own + i, strips)
        sides = []
        for e in range(2):
            onehot = (spot + which * strip == pick[e : e + 1, :]).astype(F32).astype(BF16)
            sides.append(lax.dot_general(onehot, points, nt, preferred_element_type=F32))
        both = jnp.concatenate(sides, axis=1).astype(BF16)
        going[pl.ds(which * 16, 16)] = both.reshape(16, CAP, 2 * width)

        def send(j, c):
            other = which * 16 + lax.rem(chip + j, 16)

            @pl.when(other != chip)
            def _():
                remote(going.at[other], come.at[chip], s2.at[0], r2.at[0], other * 2 + core, h).start()

            return c

        lax.fori_loop(0, 16, send, 0)
        return carry

    lax.fori_loop(0, strips, sort, 0)
    stay = pltpu.make_async_copy(going.at[chip], come.at[chip], local.at[2])
    stay.start()

    pltpu.make_async_copy(places.at[:, pl.ds(0, lines)], places.at[:, pl.ds(0, lines)], local.at[3]).wait()
    run = jnp.zeros((chips, 1), F32)
    for line in range(lines):
        row = pv[line]
        mask = jnp.where((row >> bits) == s, 1.0, 0.0)
        counts = jnp.dot(mask.astype(BF16), tri[...], preferred_element_type=F32) + run
        run = counts[:, lanes - 1 :]
        land[line] = jnp.where(mask > 0, counts - 1.0, -1.0)
        flat[line] = ((row & (rows - 1)) + 1).astype(F32)
    for low in range(0, chips, 8):
        ranks = [land[line, low : low + 8, :] for line in range(lines)]
        spots = [flat[line, low : low + 8, :] for line in range(lines)]

        def settle(k, carry):
            rank = k.astype(F32)
            total = jnp.zeros((8, lanes), F32)
            for line in range(lines):
                total += jnp.where(ranks[line] == rank, spots[line], 0.0)
            place = jnp.sum(total, axis=1, keepdims=True)
            found[pl.ds(pl.multiple_of(k * chips + low, 8), 8), :] = jnp.broadcast_to(place, (8, lanes))
            return carry

        lax.fori_loop(0, 2 * CAP, settle, 0, unroll=8)
    where = lax.broadcasted_iota(jnp.int32, (chips, lanes), 1).astype(F32) + 1.0

    def turn(k, carry):
        span = pl.ds(pl.multiple_of(k * chips, 16), chips)
        spots = found[span, :]
        for low in range(0, rows, lanes):
            turned[span, low : low + lanes] = (spots == where + float(low)).astype(F32).astype(BF16)
        return carry

    lax.fori_loop(0, 2 * CAP, turn, 0, unroll=2)

    stay.wait()
    many = pl.ds(0, chips - 1)
    every = remote(going.at[many], come.at[many], s2.at[0], r2.at[0], sibling, h)
    every.wait_recv()
    arrived = come[...].astype(F32)
    parts = []
    for k in range(0, CAP, 2):
        two = jnp.concatenate([arrived[:, k, :], arrived[:, k + 1, :]], axis=0)
        parts.append(two.T.astype(BF16))
    packed = jnp.concatenate(parts, axis=1)
    half = CAP * chips
    total = jnp.dot(packed[:width], turned[:half, :], preferred_element_type=F32)
    total += jnp.dot(packed[width:], turned[half:, :], preferred_element_type=F32)
    out[...] = total.astype(BF16)
    swap.wait_send()
    every.wait_send()


def change_order(x, places):
    width, rows = x.shape
    chips, lines, lanes = places.shape
    dma = pltpu.SemaphoreType.DMA
    return pl.pallas_call(
        order_kernel,
        out_shape=jax.ShapeDtypeStruct((width, rows), BF16),
        in_specs=[pl.BlockSpec(memory_space=pl.ANY)] * 2,
        out_specs=pl.BlockSpec(memory_space=pltpu.VMEM),
        scratch_shapes=[
            pltpu.VMEM((lines, chips, lanes), jnp.int32),
            pltpu.VMEM((lines, lanes), jnp.int32),
            pltpu.VMEM((2, width, rows), BF16),
            pltpu.VMEM((lanes, lanes), BF16),
            pltpu.VMEM((2, 2 * rows), jnp.int32),
            pltpu.VMEM((chips, CAP, 2 * width), BF16),
            pltpu.VMEM((chips, CAP, 2 * width), BF16),
            pltpu.VMEM((lines, chips, lanes), F32),
            pltpu.VMEM((lines, chips, lanes), F32),
            pltpu.VMEM((2 * CAP * chips, lanes), F32),
            pltpu.VMEM((2 * CAP * chips, rows), BF16),
            dma((4,)),
            dma((1,)),
            dma((1,)),
            dma((1,)),
            dma((1,)),
        ],
        compiler_params=pltpu.CompilerParams(
            collective_id=2, has_side_effects=True, vmem_limit_bytes=60 * 2**20
        ),
        name="change_order",
    )(x, places)


def body(groups, side, features, neighbours, valid, conv_weight, attn_weight, proj_weight, hilbert_place):
    rows = hilbert_place.shape[0]
    rest = (jnp.swapaxes(neighbours, 0, 1), valid, conv_weight, attn_weight, proj_weight)
    first, places = run_block(0, groups, features, *rest, hilbert_place.reshape(rows // 128, 128), side)
    moved = change_order(first, places.reshape(side * side, rows // 64, 128))
    return run_block(1, groups, moved, *rest)[0]


def solution(mesh):
    in_specs = (
        P("head", "seq"),
        P(None, None, "seq"),
        P(None, "seq"),
        P(None, None, "head", None),
        P(None, None, "head", None),
        P(None, "head", None),
        P("seq"),
    )
    out_specs = P("head", "seq")
    return jax.shard_map(
        functools.partial(body, mesh.shape["head"], math.isqrt(mesh.shape["seq"] // 2)),
        mesh=mesh,
        in_specs=in_specs,
        out_specs=out_specs,
        check_vma=False,
    )
```

```python
import functools
import math

import jax
import jax.numpy as jnp
from jax import lax
from jax.experimental import pallas as pl
from jax.experimental.pallas import tpu as pltpu
from jax.sharding import PartitionSpec as P

HD = 16
REACH = 256
TAPS = 27
CAP = 16
LANES = 128
MESH = pl.DeviceIdType.MESH
BF16 = jnp.bfloat16
F32 = jnp.float32


def remote(src, dst, send, recv, s, h):
    return pltpu.make_async_remote_copy(
        src_ref=src,
        dst_ref=dst,
        send_sem=send,
        recv_sem=recv,
        device_id=(s, h),
        device_id_type=MESH,
    )


def kernel(
    x,
    nbr,
    valid,
    cw,
    aw,
    pw,
    place,
    out,
    tables,
    mixes,
    heads_out,
    nb,
    vm,
    w,
    a,
    p,
    pt,
    y,
    kt,
    qm,
    va,
    places,
    pv,
    feats,
    tri,
    pick,
    going,
    come,
    land,
    flat,
    found,
    turned,
    moved,
    local,
    s1,
    r1,
    s2,
    r2,
    s3,
    r3,
    s4,
    r4,
    s5,
    r5,
    s6,
    r6,
    s7,
    r7,
    s8,
    r8,
    s9,
    r9,
    s10,
    r10,
):
    width, rows = out.shape
    heads = width // HD
    groups = lax.axis_size("head")
    shards = lax.axis_size("seq")
    side = places.shape[0]
    chips = side * side
    lines = 2 * places.shape[3]
    blocks = rows // REACH
    bits = rows.bit_length() - 1
    s = lax.axis_index("seq")
    h = lax.axis_index("head")
    core = lax.rem(s, 2)
    chip = s // 2
    zz = chip // side
    yy = lax.rem(chip, side)
    sibling = s + 1 - 2 * core
    after = lax.rem(s + 1, shards)
    before = lax.rem(s + shards - 1, shards)
    peers = [lax.rem(h + d, groups) for d in range(1, groups)]
    froms = [lax.rem(h + groups - d, groups) for d in range(1, groups)]
    sends = []

    def part(index, size=width, extra=0):
        return pl.ds(pl.multiple_of(index * width + extra, 16), size)

    mine = part(h)

    def ship(copy):
        copy.start()
        sends.append(copy)

    barrier = pltpu.get_barrier_semaphore()

    def greet(i, carry):
        other = lax.rem(chip + i, chips) * 2 + core
        pl.semaphore_signal(barrier, inc=1, device_id=(other, h), device_id_type=MESH)
        return carry

    for other in peers:
        pl.semaphore_signal(barrier, inc=1, device_id=(s, other), device_id_type=MESH)
    for other in (before, after):
        pl.semaphore_signal(barrier, inc=1, device_id=(other, h), device_id_type=MESH)
    lax.fori_loop(1, chips, greet, 0)
    loads = [
        pltpu.make_async_copy(x, tables.at[0, mine, pl.ds(REACH, rows)], local.at[0]),
        pltpu.make_async_copy(cw, w, local.at[1]),
        pltpu.make_async_copy(nbr, nb, local.at[2]),
        pltpu.make_async_copy(valid, vm, local.at[3]),
        pltpu.make_async_copy(aw, a, local.at[4]),
        pltpu.make_async_copy(pw, p.at[:, mine, :], local.at[5]),
        pltpu.make_async_copy(place, places.at[zz, yy, core], local.at[6]),
    ]
    for load in loads:
        load.start()
    low = lax.broadcasted_iota(jnp.int32, (LANES, LANES), 0)
    high = lax.broadcasted_iota(jnp.int32, (LANES, LANES), 1)
    tri[...] = jnp.where(low <= high, 1.0, 0.0).astype(BF16)
    position = lax.broadcasted_iota(jnp.int32, (REACH, REACH), 0).astype(F32).astype(BF16)
    one, zero = jnp.ones((), BF16), jnp.zeros((), BF16)
    ones = jnp.where(lax.broadcasted_iota(jnp.int32, (HD, rows), 0) == 0, 1.0, 0.0).astype(BF16)
    qm[...] = jnp.zeros(qm.shape, BF16)
    for hd in range(heads):
        qm[hd, width : width + HD, :] = ones
        va[hd, HD:, :] = ones
    pl.semaphore_wait(barrier, chips - 1 + groups - 1 + 2)

    order = (0, blocks - 1, *range(1, blocks - 1))

    def gather_start(b, source):
        for j in order:
            for d, other in enumerate(peers):
                span = pl.ds(REACH + j * REACH, REACH)
                ship(
                    remote(
                        source.at[:, pl.ds(j * REACH, REACH)],
                        tables.at[b, mine, span],
                        s1.at[b, j, d],
                        r1.at[b, j, d],
                        s,
                        other,
                    )
                )

    def gather_wait(b, j):
        for d, other in enumerate(froms):
            theirs = tables.at[b, part(other), pl.ds(REACH + j * REACH, REACH)]
            remote(theirs, theirs, s1.at[b, j, d], r1.at[b, j, d], s, other).wait_recv()

    def places_along_z():
        for d in range(1, side):
            other = (lax.rem(zz + d, side) * side + yy) * 2 + core
            ship(remote(place, places.at[zz, yy, core], s6.at[d - 1], r6.at[d - 1], other, h))

    def places_along_y():
        loads[6].wait()
        for d in range(1, side):
            theirs = places.at[lax.rem(zz + side - d, side), yy, core]
            remote(theirs, theirs, s6.at[d - 1], r6.at[d - 1], s, h).wait_recv()
        for d in range(1, side):
            other = (zz * side + lax.rem(yy + d, side)) * 2 + core
            column = places.at[:, yy, core]
            ship(remote(column, column, s7.at[d - 1], r7.at[d - 1], other, h))

    def places_across():
        for d in range(1, side):
            theirs = places.at[:, lax.rem(yy + side - d, side), core]
            remote(theirs, theirs, s7.at[d - 1], r7.at[d - 1], s, h).wait_recv()
        column = places.at[:, :, core]
        ship(remote(column, column, s8.at[0], r8.at[0], sibling, h))

    def places_finish():
        theirs = places.at[:, :, 1 - core]
        remote(theirs, theirs, s8.at[0], r8.at[0], sibling, h).wait_recv()
        for line in range(lines):
            pltpu.make_async_copy(
                places.at[:, :, line // (lines // 2), line % (lines // 2)], pv.at[line], local.at[7]
            ).start()

    def weights_start():
        loads[5].wait()
        for d, other in enumerate(peers):
            ship(remote(p.at[:, mine, :], p.at[:, mine, :], s5.at[d], r5.at[d], s, other))

    def weights_finish():
        for d, other in enumerate(froms):
            theirs = p.at[:, part(other), :]
            remote(theirs, theirs, s5.at[d], r5.at[d], s, other).wait_recv()
        for b in range(2):
            pt[b] = p[b].astype(F32).T.astype(BF16)

    def run_block(b):
        table = tables.at[b]
        mix = mixes.at[b]
        ho = heads_out.at[b]
        gather_wait(b, 0)
        first = remote(
            table.at[:, pl.ds(REACH, REACH)],
            table.at[:, pl.ds(REACH + rows, REACH)],
            s2.at[b, 0],
            r2.at[b, 0],
            before,
            h,
        )
        ship(first)
        gather_wait(b, blocks - 1)
        last = remote(
            table.at[:, pl.ds(rows, REACH)],
            table.at[:, pl.ds(0, REACH)],
            s2.at[b, 1],
            r2.at[b, 1],
            after,
            h,
        )
        ship(last)
        if b == 0:
            for load in loads[1:5]:
                load.wait()
        taps = w[b].reshape(TAPS * width, -1)

        def products(tile):
            points = table[:, tile * REACH : (tile + 1) * REACH]
            value = jnp.dot(taps, points, preferred_element_type=F32).astype(BF16)
            y[:, tile] = value.reshape(TAPS, width, REACH)

        def conv(blk):
            cols = slice(blk * REACH, (blk + 1) * REACH)
            base = s * rows + (blk - 1) * REACH
            total = jnp.zeros((width, REACH), F32)
            for t in range(TAPS):
                index = nb[t, b : b + 1, cols]
                spot = index - base
                tile = jnp.where(index < 0, 3, spot >> 8)
                within = (spot & (REACH - 1)).astype(F32).astype(BF16)
                chosen = jnp.where(position == within, one, zero)
                terms = y[t, blk : blk + 3].reshape(3 * width, REACH)
                picked = jnp.dot(terms, chosen, preferred_element_type=F32)
                term = jnp.where(tile == 0, picked[:width], 0.0)
                term = jnp.where(tile == 1, picked[width : 2 * width], term)
                term = jnp.where(tile == 2, picked[2 * width :], term)
                total = total + term
            own = table[mine, REACH + blk * REACH : REACH + (blk + 1) * REACH].astype(F32)
            mix[mine, cols] = (own + total).astype(BF16)
            for d, other in enumerate(peers):
                ship(remote(mix.at[mine, cols], mix.at[mine, cols], s3.at[b, blk, d], r3.at[b, blk, d], s, other))

        products(1)
        products(blocks)
        for tile in range(2, blocks):
            gather_wait(b, tile - 1)
            products(tile)
        for blk in range(1, blocks - 1):
            conv(blk)
        if b == 0:
            places_along_y()
        last.wait_recv()
        products(0)
        conv(0)
        first.wait_recv()
        products(blocks + 1)
        conv(blocks - 1)
        if b == 0:
            weights_start()
            places_across()

        scale = 1.0 / HD**0.5
        bias = jnp.where(vm[b : b + 1, :] > 0, 0.0, -1e30)
        weights = a[b].reshape(3 * width, -1)
        for blk in (*range(1, blocks - 1), 0, blocks - 1):
            cols = slice(blk * REACH, (blk + 1) * REACH)
            for d, other in enumerate(froms):
                theirs = mix.at[part(other), cols]
                remote(theirs, theirs, s3.at[b, blk, d], r3.at[b, blk, d], s, other).wait_recv()
            values = mix[:, cols].astype(F32)
            centred = values - jnp.mean(values, axis=0, keepdims=True)
            variance = jnp.mean(centred * centred, axis=0, keepdims=True)
            normed = (centred * lax.rsqrt(variance + 1e-05)).astype(BF16)
            qkv = jnp.dot(weights, normed, preferred_element_type=F32)
            query = (qkv[:width].astype(BF16).astype(F32) * scale).astype(BF16)
            value = qkv[2 * width :].astype(BF16)
            for hd in range(heads):
                span = slice(hd * HD, (hd + 1) * HD)
                qm[hd, span, cols] = query[span]
                va[hd, :HD, cols] = value[span]
            tail = jnp.where(
                lax.broadcasted_iota(jnp.int32, (width, REACH), 0) == 0, bias[:, cols], 0.0
            )
            keys = jnp.concatenate([qkv[width : 2 * width], tail], axis=0)
            kt[cols, :] = keys.T.astype(BF16)

        for hd in range(heads):
            scores = jnp.dot(kt[...], qm[hd], preferred_element_type=F32)
            top = jnp.max(scores, axis=0, keepdims=True)
            probs = jnp.exp((scores - top).astype(BF16))
            summed = jnp.dot(va[hd], probs, preferred_element_type=F32)
            result = summed[:HD] / summed[HD : HD + 1]
            span = part(h, HD, hd * HD)
            ho[span, :] = result.astype(BF16)
            for d, other in enumerate(peers):
                ship(remote(ho.at[span, :], ho.at[span, :], s4.at[b, hd, d], r4.at[b, hd, d], s, other))

    def project(b):
        mix = mixes.at[b]
        ho = heads_out.at[b]
        for hd in range(heads):
            for d, other in enumerate(froms):
                theirs = ho.at[part(other, HD, hd * HD), :]
                remote(theirs, theirs, s4.at[b, hd, d], r4.at[b, hd, d], s, other).wait_recv()
        update = jnp.dot(pt[b, mine, :], ho[...], preferred_element_type=F32)
        return (mix[mine, :].astype(F32) + update).astype(BF16)

    gather_start(0, x)
    places_along_z()
    loads[0].wait()
    run_block(0)

    weights_finish()
    places_finish()
    column = lax.broadcasted_iota(jnp.int32, (chips, LANES), 0)
    run = jnp.zeros((chips, 1), F32)
    slots = []
    for line in range(lines):
        half = lines // 2
        row = places[zz, yy, line // half, line % half : line % half + 1, :]
        device = row >> bits
        mask = jnp.where(device == column * 2 + core, 1.0, 0.0)
        counts = jnp.dot(mask.astype(BF16), tri[...], preferred_element_type=F32) + run
        run = counts[:, LANES - 1 :]
        rank = (jnp.sum(mask * counts, axis=0, keepdims=True) - 1.0).astype(jnp.int32)
        here = (device & 1) == core
        target = (device >> 1) * CAP + (rank & (CAP - 1))
        slots.append((jnp.where(here, target, -1), rank >> 4))
    targets = jnp.concatenate([t for t, _ in slots], axis=1)
    halves = jnp.concatenate([e for _, e in slots], axis=1)
    for e in range(2):
        pick[e : e + 1, :] = jnp.where(halves == e, targets, -1)

    feats[core] = project(0)
    swap = remote(feats.at[core], feats.at[core], s9.at[0], r9.at[0], sibling, h)
    ship(swap)
    theirs = feats.at[1 - core]
    remote(theirs, theirs, s9.at[0], r9.at[0], sibling, h).wait_recv()
    points = jnp.concatenate([feats[0], feats[1]], axis=1)
    batch = 16
    strip = batch * CAP
    strips = chips // batch
    own = chip // batch
    spot = lax.broadcasted_iota(jnp.int32, (strip, 2 * rows), 0)
    nt = (((1,), (1,)), ((), ()))

    def sort(i, carry):
        which = lax.rem(own + i, strips)
        sides = []
        for e in range(2):
            onehot = (spot + which * strip == pick[e : e + 1, :]).astype(F32).astype(BF16)
            sides.append(lax.dot_general(onehot, points, nt, preferred_element_type=F32))
        both = jnp.concatenate(sides, axis=1).astype(BF16)
        going[pl.ds(which * batch, batch)] = both.reshape(batch, CAP, 2 * width)

        def send(j, c):
            other = which * batch + lax.rem(chip + j, batch)

            @pl.when(other != chip)
            def _():
                remote(going.at[other], come.at[chip], s10.at[0], r10.at[0], other * 2 + core, h).start()

            return c

        lax.fori_loop(0, batch, send, 0)
        return carry

    lax.fori_loop(0, strips, sort, 0)
    stay = pltpu.make_async_copy(going.at[chip], come.at[chip], local.at[8])
    stay.start()

    pltpu.make_async_copy(pv, pv, local.at[7]).wait()
    run = jnp.zeros((chips, 1), F32)
    for line in range(lines):
        row = pv[line].reshape(chips, LANES)
        mask = jnp.where((row >> bits) == s, 1.0, 0.0)
        counts = jnp.dot(mask.astype(BF16), tri[...], preferred_element_type=F32) + run
        run = counts[:, LANES - 1 :]
        land[line] = jnp.where(mask > 0, counts - 1.0, -1.0)
        flat[line] = ((row & (rows - 1)) + 1).astype(F32)
    for start in range(0, chips, 8):
        ranks = [land[line, start : start + 8, :] for line in range(lines)]
        spots = [flat[line, start : start + 8, :] for line in range(lines)]

        def settle(k, carry):
            rank = k.astype(F32)
            total = jnp.zeros((8, LANES), F32)
            for line in range(lines):
                total += jnp.where(ranks[line] == rank, spots[line], 0.0)
            where = jnp.sum(total, axis=1, keepdims=True)
            found[pl.ds(pl.multiple_of(k * chips + start, 8), 8), :] = jnp.broadcast_to(where, (8, LANES))
            return carry

        lax.fori_loop(0, 2 * CAP, settle, 0, unroll=8)
    lane = lax.broadcasted_iota(jnp.int32, (chips, LANES), 1).astype(F32) + 1.0

    def turn(k, carry):
        span = pl.ds(pl.multiple_of(k * chips, 16), chips)
        spots = found[span, :]
        for start in range(0, rows, LANES):
            turned[span, start : start + LANES] = (spots == lane + float(start)).astype(F32).astype(BF16)
        return carry

    lax.fori_loop(0, 2 * CAP, turn, 0, unroll=2)

    stay.wait()
    many = pl.ds(0, chips - 1)
    every = remote(going.at[many], come.at[many], s10.at[0], r10.at[0], sibling, h)
    every.wait_recv()
    arrived = come[...].astype(F32)
    parts = []
    for k in range(0, CAP, 2):
        two = jnp.concatenate([arrived[:, k, :], arrived[:, k + 1, :]], axis=0)
        parts.append(two.T.astype(BF16))
    packed = jnp.concatenate(parts, axis=1)
    half = CAP * chips
    total = jnp.dot(packed[:width], turned[:half, :], preferred_element_type=F32)
    total += jnp.dot(packed[width:], turned[half:, :], preferred_element_type=F32)
    moved[...] = total.astype(BF16)
    gather_start(1, moved)
    tables[1, mine, REACH : REACH + rows] = moved[...]
    run_block(1)
    out[...] = project(1)
    for copy in sends:
        copy.wait_send()
    every.wait_send()


def body(groups, side, features, neighbours, valid, conv_weight, attn_weight, proj_weight, hilbert_place):
    width, rows = features.shape
    channels = width * groups
    heads = width // HD
    blocks = rows // REACH
    chips = side * side
    lines = 2 * rows // LANES
    others = groups - 1
    dma = pltpu.SemaphoreType.DMA
    vmem = pltpu.VMEM
    pairs = [(2, blocks, others), (2, 2), (2, blocks, others), (2, heads, others), (others,)]
    pairs += [(side - 1,), (side - 1,), (1,), (1,), (1,)]
    return pl.pallas_call(
        kernel,
        out_shape=jax.ShapeDtypeStruct((width, rows), BF16),
        in_specs=[pl.BlockSpec(memory_space=pl.ANY)] * 7,
        out_specs=pl.BlockSpec(memory_space=pltpu.VMEM),
        scratch_shapes=[
            vmem((2, channels, rows + 2 * REACH), BF16),
            vmem((2, channels, rows), BF16),
            vmem((2, channels, rows), BF16),
            vmem((TAPS, 2, rows), jnp.int32),
            vmem((2, rows), jnp.int32),
            vmem((2, TAPS, width, channels), BF16),
            vmem((2, 3, width, channels), BF16),
            vmem((2, channels, channels), BF16),
            vmem((2, channels, channels), BF16),
            vmem((TAPS, blocks + 2, width, REACH), BF16),
            vmem((rows, 2 * width), BF16),
            vmem((heads, 2 * width, rows), BF16),
            vmem((heads, 2 * HD, rows), BF16),
            vmem((side, side, 2, rows // LANES, LANES), jnp.int32),
            vmem((lines, side, side, LANES), jnp.int32),
            vmem((2, width, rows), BF16),
            vmem((LANES, LANES), BF16),
            vmem((2, 2 * rows), jnp.int32),
            vmem((chips, CAP, 2 * width), BF16),
            vmem((chips, CAP, 2 * width), BF16),
            vmem((lines, chips, LANES), F32),
            vmem((lines, chips, LANES), F32),
            vmem((2 * CAP * chips, LANES), F32),
            vmem((2 * CAP * chips, rows), BF16),
            vmem((width, rows), BF16),
            dma((9,)),
            *[dma(shape) for shape in pairs for _ in range(2)],
        ],
        compiler_params=pltpu.CompilerParams(
            collective_id=0, has_side_effects=True, vmem_limit_bytes=60 * 2**20
        ),
        name="blocks",
    )(
        features,
        jnp.swapaxes(neighbours, 0, 1),
        valid,
        conv_weight,
        attn_weight,
        proj_weight,
        hilbert_place.reshape(rows // LANES, LANES),
    )


def solution(mesh):
    in_specs = (
        P("head", "seq"),
        P(None, None, "seq"),
        P(None, "seq"),
        P(None, None, "head", None),
        P(None, None, "head", None),
        P(None, "head", None),
        P("seq"),
    )
    return jax.shard_map(
        functools.partial(body, mesh.shape["head"], math.isqrt(mesh.shape["seq"] // 2)),
        mesh=mesh,
        in_specs=in_specs,
        out_specs=P("head", "seq"),
        check_vma=False,
    )
```

```python
import functools
import math

import jax
import jax.numpy as jnp
from jax import lax
from jax.experimental import pallas as pl
from jax.experimental.pallas import tpu as pltpu
from jax.sharding import PartitionSpec as P

HD = 16
REACH = 256
TAPS = 27
CAP = 16
LANES = 128
MESH = pl.DeviceIdType.MESH
BF16 = jnp.bfloat16
F32 = jnp.float32


def remote(src, dst, send, recv, s, h):
    return pltpu.make_async_remote_copy(
        src_ref=src,
        dst_ref=dst,
        send_sem=send,
        recv_sem=recv,
        device_id=(s, h),
        device_id_type=MESH,
    )


def kernel(
    x,
    nbr,
    valid,
    cw,
    aw,
    pw,
    place,
    out,
    tables,
    mixes,
    heads_out,
    nb,
    vm,
    w,
    a,
    p,
    pq,
    pall,
    pt,
    y,
    kt,
    qm,
    va,
    places,
    pv,
    feats,
    tri,
    onehot,
    partial,
    going,
    come,
    land,
    flat,
    found,
    turned,
    moved,
    local,
    s1,
    r1,
    s2,
    r2,
    s3,
    r3,
    s4,
    r4,
    s5,
    r5,
    s6,
    r6,
    s7,
    r7,
    s8,
    r8,
    s9,
    r9,
    s10,
    r10,
):
    width, rows = out.shape
    heads = width // HD
    groups = lax.axis_size("head")
    shards = lax.axis_size("seq")
    side = places.shape[0]
    chips = side * side
    lines = 2 * places.shape[3]
    blocks = rows // REACH
    bits = rows.bit_length() - 1
    s = lax.axis_index("seq")
    h = lax.axis_index("head")
    core = lax.rem(s, 2)
    chip = s // 2
    zz = chip // side
    yy = lax.rem(chip, side)
    sibling = s + 1 - 2 * core
    after = lax.rem(s + 1, shards)
    before = lax.rem(s + shards - 1, shards)
    peers = [lax.rem(h + d, groups) for d in range(1, groups)]
    froms = [lax.rem(h + groups - d, groups) for d in range(1, groups)]
    sends = []

    def part(index, size=width, extra=0):
        return pl.ds(pl.multiple_of(index * width + extra, 16), size)

    mine = part(h)

    def ship(copy):
        copy.start()
        sends.append(copy)

    barrier = pltpu.get_barrier_semaphore()

    def greet(i, carry):
        other = lax.rem(chip + i, chips) * 2 + core
        pl.semaphore_signal(barrier, inc=1, device_id=(other, h), device_id_type=MESH)
        return carry

    for other in peers:
        pl.semaphore_signal(barrier, inc=1, device_id=(s, other), device_id_type=MESH)
    for other in (before, after):
        pl.semaphore_signal(barrier, inc=1, device_id=(other, h), device_id_type=MESH)
    lax.fori_loop(1, chips, greet, 0)
    loads = [
        pltpu.make_async_copy(x, tables.at[0, mine, pl.ds(REACH, rows)], local.at[0]),
        pltpu.make_async_copy(cw, w, local.at[1]),
        pltpu.make_async_copy(nbr, nb, local.at[2]),
        pltpu.make_async_copy(valid, vm, local.at[3]),
        pltpu.make_async_copy(aw, a, local.at[4]),
        pltpu.make_async_copy(pw, p, local.at[5]),
        pltpu.make_async_copy(place, places.at[zz, yy, core], local.at[6]),
    ]
    for load in loads:
        load.start()
    low = lax.broadcasted_iota(jnp.int32, (LANES, LANES), 0)
    high = lax.broadcasted_iota(jnp.int32, (LANES, LANES), 1)
    tri[...] = jnp.where(low <= high, 1.0, 0.0).astype(BF16)
    position = lax.broadcasted_iota(jnp.int32, (REACH, REACH), 0).astype(F32).astype(BF16)
    one, zero = jnp.ones((), BF16), jnp.zeros((), BF16)
    ones = jnp.where(lax.broadcasted_iota(jnp.int32, (HD, rows), 0) == 0, 1.0, 0.0).astype(BF16)
    qm[...] = jnp.zeros(qm.shape, BF16)
    for hd in range(heads):
        qm[hd, width : width + HD, :] = ones
        va[hd, HD:, :] = ones
    pl.semaphore_wait(barrier, chips - 1 + groups - 1 + 2)

    order = (0, blocks - 1, *range(1, blocks - 1))

    def gather_piece(b, source, j):
        for d, other in enumerate(peers):
            span = pl.ds(REACH + j * REACH, REACH)
            ship(
                remote(
                    source.at[:, pl.ds(j * REACH, REACH)],
                    tables.at[b, mine, span],
                    s1.at[b, j, d],
                    r1.at[b, j, d],
                    s,
                    other,
                )
            )

    def gather_wait(b, j):
        for d, other in enumerate(froms):
            theirs = tables.at[b, part(other), pl.ds(REACH + j * REACH, REACH)]
            remote(theirs, theirs, s1.at[b, j, d], r1.at[b, j, d], s, other).wait_recv()

    def places_along_z():
        for d in range(1, side):
            other = (lax.rem(zz + d, side) * side + yy) * 2 + core
            ship(remote(place, places.at[zz, yy, core], s6.at[d - 1], r6.at[d - 1], other, h))

    def places_along_y():
        loads[6].wait()
        for d in range(1, side):
            theirs = places.at[lax.rem(zz + side - d, side), yy, core]
            remote(theirs, theirs, s6.at[d - 1], r6.at[d - 1], s, h).wait_recv()
        for d in range(1, side):
            other = (zz * side + lax.rem(yy + d, side)) * 2 + core
            column = places.at[:, yy, core]
            ship(remote(column, column, s7.at[d - 1], r7.at[d - 1], other, h))

    def places_across():
        for d in range(1, side):
            theirs = places.at[:, lax.rem(yy + side - d, side), core]
            remote(theirs, theirs, s7.at[d - 1], r7.at[d - 1], s, h).wait_recv()
        column = places.at[:, :, core]
        ship(remote(column, column, s8.at[0], r8.at[0], sibling, h))

    def places_finish():
        theirs = places.at[:, :, 1 - core]
        remote(theirs, theirs, s8.at[0], r8.at[0], sibling, h).wait_recv()
        for line in range(lines):
            pltpu.make_async_copy(
                places.at[:, :, line // (lines // 2), line % (lines // 2)], pv.at[line], local.at[7]
            ).start()

    def weights_start():
        loads[5].wait()
        both = jnp.concatenate([p[0], p[1]], axis=0).astype(F32)
        pq[...] = both.T.astype(BF16)
        for d, other in enumerate(peers):
            ship(remote(pq.at[part(other), :], pall.at[h], s5.at[d], r5.at[d], s, other))
        pall[h] = pq[mine, :]

    def weights_finish():
        for d, other in enumerate(froms):
            remote(pall.at[other], pall.at[other], s5.at[d], r5.at[d], s, other).wait_recv()
        for b in range(2):
            span = slice(b * width, (b + 1) * width)
            pt[b] = jnp.concatenate([pall[g, :, span].astype(F32) for g in range(groups)], axis=1).astype(BF16)

    batch = 16
    strip = batch * CAP
    strips = chips // batch

    def prepare():
        weights_finish()
        places_finish()
        column = lax.broadcasted_iota(jnp.int32, (chips, LANES), 0)
        run = jnp.zeros((chips, 1), F32)
        half = lines // 2
        slots = []
        for line in range(lines):
            row = places[zz, yy, line // half, line % half : line % half + 1, :]
            device = row >> bits
            mask = jnp.where(device == column * 2 + core, 1.0, 0.0)
            counts = jnp.dot(mask.astype(BF16), tri[...], preferred_element_type=F32) + run
            run = counts[:, LANES - 1 :]
            rank = (jnp.sum(mask * counts, axis=0, keepdims=True) - 1.0).astype(jnp.int32)
            here = (device & 1) == core
            target = (device >> 1) * CAP + (rank & (CAP - 1))
            slots.append((jnp.where(here, target, -1), rank >> 4))
        spot = lax.broadcasted_iota(jnp.int32, (strip, rows), 0)
        for c in range(2):
            targets = jnp.concatenate([t for t, _ in slots[c * half : (c + 1) * half]], axis=1)
            halves = jnp.concatenate([e for _, e in slots[c * half : (c + 1) * half]], axis=1)
            for e in range(2):
                wanted = jnp.where(halves == e, targets, -1)
                for i in range(strips):
                    rows_of = slice(i * strip, (i + 1) * strip)
                    onehot[e, c, rows_of, :] = (spot == wanted - i * strip).astype(F32).astype(BF16)

    def run_block(b):
        table = tables.at[b]
        mix = mixes.at[b]
        ho = heads_out.at[b]
        gather_wait(b, 0)
        first = remote(
            table.at[:, pl.ds(REACH, REACH)],
            table.at[:, pl.ds(REACH + rows, REACH)],
            s2.at[b, 0],
            r2.at[b, 0],
            before,
            h,
        )
        ship(first)
        gather_wait(b, blocks - 1)
        last = remote(
            table.at[:, pl.ds(rows, REACH)],
            table.at[:, pl.ds(0, REACH)],
            s2.at[b, 1],
            r2.at[b, 1],
            after,
            h,
        )
        ship(last)
        if b == 0:
            places_along_y()
            for load in loads[1:5]:
                load.wait()
        taps = w[b].reshape(TAPS * width, -1)

        def products(tile):
            points = table[:, tile * REACH : (tile + 1) * REACH]
            value = jnp.dot(taps, points, preferred_element_type=F32).astype(BF16)
            y[:, tile] = value.reshape(TAPS, width, REACH)

        def conv(blk):
            cols = slice(blk * REACH, (blk + 1) * REACH)
            base = s * rows + (blk - 1) * REACH
            total = jnp.zeros((width, REACH), F32)
            for t in range(TAPS):
                index = nb[t, b : b + 1, cols]
                spot = index - base
                tile = jnp.where(index < 0, 3, spot >> 8)
                within = (spot & (REACH - 1)).astype(F32).astype(BF16)
                chosen = jnp.where(position == within, one, zero)
                terms = y[t, blk : blk + 3].reshape(3 * width, REACH)
                picked = jnp.dot(terms, chosen, preferred_element_type=F32)
                term = jnp.where(tile == 0, picked[:width], 0.0)
                term = jnp.where(tile == 1, picked[width : 2 * width], term)
                term = jnp.where(tile == 2, picked[2 * width :], term)
                total = total + term
            own = table[mine, REACH + blk * REACH : REACH + (blk + 1) * REACH].astype(F32)
            mix[mine, cols] = (own + total).astype(BF16)
            for d, other in enumerate(peers):
                ship(remote(mix.at[mine, cols], mix.at[mine, cols], s3.at[b, blk, d], r3.at[b, blk, d], s, other))

        products(1)
        products(blocks)
        for tile in range(2, blocks):
            gather_wait(b, tile - 1)
            products(tile)
        for blk in range(1, blocks - 1):
            conv(blk)
        if b == 0:
            places_across()
        last.wait_recv()
        products(0)
        conv(0)
        first.wait_recv()
        products(blocks + 1)
        conv(blocks - 1)
        if b == 0:
            prepare()

        scale = 1.0 / HD**0.5
        bias = jnp.where(vm[b : b + 1, :] > 0, 0.0, -1e30)
        weights = a[b].reshape(3 * width, -1)
        for blk in (*range(1, blocks - 1), 0, blocks - 1):
            cols = slice(blk * REACH, (blk + 1) * REACH)
            for d, other in enumerate(froms):
                theirs = mix.at[part(other), cols]
                remote(theirs, theirs, s3.at[b, blk, d], r3.at[b, blk, d], s, other).wait_recv()
            values = mix[:, cols].astype(F32)
            centred = values - jnp.mean(values, axis=0, keepdims=True)
            variance = jnp.mean(centred * centred, axis=0, keepdims=True)
            normed = (centred * lax.rsqrt(variance + 1e-05)).astype(BF16)
            qkv = jnp.dot(weights, normed, preferred_element_type=F32)
            query = (qkv[:width].astype(BF16).astype(F32) * scale).astype(BF16)
            value = qkv[2 * width :].astype(BF16)
            for hd in range(heads):
                span = slice(hd * HD, (hd + 1) * HD)
                qm[hd, span, cols] = query[span]
                va[hd, :HD, cols] = value[span]
            tail = jnp.where(
                lax.broadcasted_iota(jnp.int32, (width, REACH), 0) == 0, bias[:, cols], 0.0
            )
            keys = jnp.concatenate([qkv[width : 2 * width], tail], axis=0)
            kt[cols, :] = keys.T.astype(BF16)

        def score(hd):
            return jnp.dot(kt[...], qm[hd], preferred_element_type=F32)

        upcoming = score(0)
        for hd in range(heads):
            scores = upcoming
            if hd + 1 < heads:
                upcoming = score(hd + 1)
            top = jnp.max(scores, axis=0, keepdims=True)
            probs = jnp.exp(scores - top).astype(BF16)
            summed = jnp.dot(va[hd], probs, preferred_element_type=F32)
            result = summed[:HD] / summed[HD : HD + 1]
            span = part(h, HD, hd * HD)
            ho[span, :] = result.astype(BF16)
            for d, other in enumerate(peers):
                ship(remote(ho.at[span, :], ho.at[span, :], s4.at[b, hd, d], r4.at[b, hd, d], s, other))

    def project(b):
        mix = mixes.at[b]
        ho = heads_out.at[b]
        for hd in range(heads):
            for d, other in enumerate(froms):
                theirs = ho.at[part(other, HD, hd * HD), :]
                remote(theirs, theirs, s4.at[b, hd, d], r4.at[b, hd, d], s, other).wait_recv()
        update = jnp.dot(pt[b], ho[...], preferred_element_type=F32)
        return (mix[mine, :].astype(F32) + update).astype(BF16)

    for j in order:
        gather_piece(0, x, j)
    places_along_z()
    weights_start()
    loads[0].wait()
    run_block(0)

    feats[core] = project(0)
    swap = remote(feats.at[core], feats.at[core], s9.at[0], r9.at[0], sibling, h)
    ship(swap)
    own = chip // batch
    nt = (((1,), (1,)), ((), ()))

    def sorted_part(c, which):
        span = pl.ds(pl.multiple_of(which * strip, strip), strip)
        points = feats[c]
        sides = [
            lax.dot_general(onehot[e, c, span, :], points, nt, preferred_element_type=F32) for e in range(2)
        ]
        return span, jnp.concatenate(sides, axis=1)

    def sort_own(which, carry):
        span, value = sorted_part(core, which)
        partial[span, :] = value
        return carry

    lax.fori_loop(0, strips, sort_own, 0, unroll=2)
    theirs = feats.at[1 - core]
    remote(theirs, theirs, s9.at[0], r9.at[0], sibling, h).wait_recv()

    def sort(i, carry):
        which = lax.rem(own + i, strips)
        span, value = sorted_part(1 - core, which)
        both = (partial[span, :] + value).astype(BF16)
        going[pl.ds(which * batch, batch)] = both.reshape(batch, CAP, 2 * width)

        def send(j, c):
            other = which * batch + lax.rem(chip + j, batch)

            @pl.when(other != chip)
            def _():
                remote(going.at[other], come.at[chip], s10.at[0], r10.at[0], other * 2 + core, h).start()

            return c

        lax.fori_loop(0, batch, send, 0)
        return carry

    lax.fori_loop(0, strips, sort, 0)
    stay = pltpu.make_async_copy(going.at[chip], come.at[chip], local.at[8])
    stay.start()

    pltpu.make_async_copy(pv, pv, local.at[7]).wait()
    run = jnp.zeros((chips, 1), F32)
    for line in range(lines):
        row = pv[line].reshape(chips, LANES)
        mask = jnp.where((row >> bits) == s, 1.0, 0.0)
        counts = jnp.dot(mask.astype(BF16), tri[...], preferred_element_type=F32) + run
        run = counts[:, LANES - 1 :]
        land[line] = jnp.where(mask > 0, counts - 1.0, -1.0)
        flat[line] = ((row & (rows - 1)) + 1).astype(F32)
    for start in range(0, chips, 8):
        ranks = [land[line, start : start + 8, :] for line in range(lines)]
        spots = [flat[line, start : start + 8, :] for line in range(lines)]

        def settle(k, carry):
            rank = k.astype(F32)
            total = jnp.zeros((8, LANES), F32)
            for line in range(lines):
                total += jnp.where(ranks[line] == rank, spots[line], 0.0)
            where = jnp.sum(total, axis=1, keepdims=True)
            found[pl.ds(pl.multiple_of(k * chips + start, 8), 8), :] = jnp.broadcast_to(where, (8, LANES))
            return carry

        lax.fori_loop(0, 2 * CAP, settle, 0, unroll=8)
    lane = lax.broadcasted_iota(jnp.int32, (chips, LANES), 1).astype(F32) + 1.0

    def turn(k, carry):
        span = pl.ds(pl.multiple_of(k * chips, 16), chips)
        spots = found[span, :]
        for start in range(0, rows, LANES):
            turned[span, start : start + LANES] = (spots == lane + float(start)).astype(F32).astype(BF16)
        return carry

    lax.fori_loop(0, 2 * CAP, turn, 0, unroll=2)

    stay.wait()
    many = pl.ds(0, chips - 1)
    every = remote(going.at[many], come.at[many], s10.at[0], r10.at[0], sibling, h)
    every.wait_recv()
    arrived = come[...].astype(F32)
    parts = []
    for k in range(0, CAP, 2):
        two = jnp.concatenate([arrived[:, k, :], arrived[:, k + 1, :]], axis=0)
        parts.append(two.T.astype(BF16))
    packed = jnp.concatenate(parts, axis=1)
    half = CAP * chips
    for j in order:
        cols = slice(j * REACH, (j + 1) * REACH)
        total = jnp.dot(packed[:width], turned[:half, cols], preferred_element_type=F32)
        total += jnp.dot(packed[width:], turned[half:, cols], preferred_element_type=F32)
        moved[:, cols] = total.astype(BF16)
        gather_piece(1, moved, j)
    tables[1, mine, REACH : REACH + rows] = moved[...]
    run_block(1)
    out[...] = project(1)
    for copy in sends:
        copy.wait_send()
    every.wait_send()


def body(groups, side, features, neighbours, valid, conv_weight, attn_weight, proj_weight, hilbert_place):
    width, rows = features.shape
    channels = width * groups
    heads = width // HD
    blocks = rows // REACH
    chips = side * side
    lines = 2 * rows // LANES
    others = groups - 1
    dma = pltpu.SemaphoreType.DMA
    vmem = pltpu.VMEM
    pairs = [(2, blocks, others), (2, 2), (2, blocks, others), (2, heads, others), (others,)]
    pairs += [(side - 1,), (side - 1,), (1,), (1,), (1,)]
    return pl.pallas_call(
        kernel,
        out_shape=jax.ShapeDtypeStruct((width, rows), BF16),
        in_specs=[pl.BlockSpec(memory_space=pl.ANY)] * 7,
        out_specs=pl.BlockSpec(memory_space=pltpu.VMEM),
        scratch_shapes=[
            vmem((2, channels, rows + 2 * REACH), BF16),
            vmem((2, channels, rows), BF16),
            vmem((2, channels, rows), BF16),
            vmem((TAPS, 2, rows), jnp.int32),
            vmem((2, rows), jnp.int32),
            vmem((2, TAPS, width, channels), BF16),
            vmem((2, 3, width, channels), BF16),
            vmem((2, width, channels), BF16),
            vmem((channels, 2 * width), BF16),
            vmem((groups, width, 2 * width), BF16),
            vmem((2, width, channels), BF16),
            vmem((TAPS, blocks + 2, width, REACH), BF16),
            vmem((rows, 2 * width), BF16),
            vmem((heads, 2 * width, rows), BF16),
            vmem((heads, 2 * HD, rows), BF16),
            vmem((side, side, 2, rows // LANES, LANES), jnp.int32),
            vmem((lines, side, side, LANES), jnp.int32),
            vmem((2, width, rows), BF16),
            vmem((LANES, LANES), BF16),
            vmem((2, 2, chips * CAP, rows), BF16),
            vmem((chips * CAP, 2 * width), F32),
            vmem((chips, CAP, 2 * width), BF16),
            vmem((chips, CAP, 2 * width), BF16),
            vmem((lines, chips, LANES), F32),
            vmem((lines, chips, LANES), F32),
            vmem((2 * CAP * chips, LANES), F32),
            vmem((2 * CAP * chips, rows), BF16),
            vmem((width, rows), BF16),
            dma((9,)),
            *[dma(shape) for shape in pairs for _ in range(2)],
        ],
        compiler_params=pltpu.CompilerParams(
            collective_id=0, has_side_effects=True, vmem_limit_bytes=60 * 2**20
        ),
        name="blocks",
    )(
        features,
        jnp.swapaxes(neighbours, 0, 1),
        valid,
        conv_weight,
        attn_weight,
        proj_weight,
        hilbert_place.reshape(rows // LANES, LANES),
    )


def solution(mesh):
    in_specs = (
        P("head", "seq"),
        P(None, None, "seq"),
        P(None, "seq"),
        P(None, None, "head", None),
        P(None, None, "head", None),
        P(None, "head", None),
        P("seq"),
    )
    return jax.shard_map(
        functools.partial(body, mesh.shape["head"], math.isqrt(mesh.shape["seq"] // 2)),
        mesh=mesh,
        in_specs=in_specs,
        out_specs=P("head", "seq"),
        check_vma=False,
    )
```

```python
import functools
import math

import jax
import jax.numpy as jnp
from jax import lax
from jax.experimental import pallas as pl
from jax.experimental.pallas import tpu as pltpu
from jax.sharding import PartitionSpec as P

HD = 16
REACH = 256
TAPS = 27
CAP = 16
LANES = 128
MESH = pl.DeviceIdType.MESH
BF16 = jnp.bfloat16
F32 = jnp.float32


def remote(src, dst, send, recv, s, h):
    return pltpu.make_async_remote_copy(
        src_ref=src,
        dst_ref=dst,
        send_sem=send,
        recv_sem=recv,
        device_id=(s, h),
        device_id_type=MESH,
    )


def kernel(
    x,
    nbr,
    valid,
    cw,
    aw,
    pw,
    place,
    out,
    tables,
    mixes,
    heads_out,
    nb,
    vm,
    w,
    a,
    p,
    pq,
    pall,
    pt,
    y,
    kt,
    qm,
    va,
    places,
    pv,
    feats,
    tri,
    onehot,
    side_of,
    turned_feats,
    partial,
    going,
    come,
    land,
    flat,
    found,
    turned,
    moved,
    local,
    s1,
    r1,
    s2,
    r2,
    s3,
    r3,
    s4,
    r4,
    s5,
    r5,
    s6,
    r6,
    s7,
    r7,
    s8,
    r8,
    s9,
    r9,
    s10,
    r10,
):
    width, rows = out.shape
    heads = width // HD
    groups = lax.axis_size("head")
    shards = lax.axis_size("seq")
    side = places.shape[0]
    chips = side * side
    lines = 2 * places.shape[3]
    blocks = rows // REACH
    bits = rows.bit_length() - 1
    s = lax.axis_index("seq")
    h = lax.axis_index("head")
    core = lax.rem(s, 2)
    chip = s // 2
    zz = chip // side
    yy = lax.rem(chip, side)
    sibling = s + 1 - 2 * core
    after = lax.rem(s + 1, shards)
    before = lax.rem(s + shards - 1, shards)
    peers = [lax.rem(h + d, groups) for d in range(1, groups)]
    froms = [lax.rem(h + groups - d, groups) for d in range(1, groups)]
    sends = []

    def part(index, size=width, extra=0):
        return pl.ds(pl.multiple_of(index * width + extra, 16), size)

    mine = part(h)

    def ship(copy):
        copy.start()
        sends.append(copy)

    barrier = pltpu.get_barrier_semaphore()

    def greet(i, carry):
        other = lax.rem(chip + i, chips) * 2 + core
        pl.semaphore_signal(barrier, inc=1, device_id=(other, h), device_id_type=MESH)
        return carry

    for other in peers:
        pl.semaphore_signal(barrier, inc=1, device_id=(s, other), device_id_type=MESH)
    for other in (before, after):
        pl.semaphore_signal(barrier, inc=1, device_id=(other, h), device_id_type=MESH)
    lax.fori_loop(1, chips, greet, 0)
    loads = [
        pltpu.make_async_copy(x, tables.at[0, mine, pl.ds(REACH, rows)], local.at[0]),
        pltpu.make_async_copy(cw, w, local.at[1]),
        pltpu.make_async_copy(nbr, nb, local.at[2]),
        pltpu.make_async_copy(valid, vm, local.at[3]),
        pltpu.make_async_copy(aw, a, local.at[4]),
        pltpu.make_async_copy(pw, p, local.at[5]),
        pltpu.make_async_copy(place, places.at[zz, yy, core], local.at[6]),
    ]
    for load in loads:
        load.start()
    pl.semaphore_wait(barrier, chips - 1 + groups - 1 + 2)

    def gather_piece(b, source, j):
        for d, other in enumerate(peers):
            span = pl.ds(REACH + j * REACH, REACH)
            ship(
                remote(
                    source.at[:, pl.ds(j * REACH, REACH)],
                    tables.at[b, mine, span],
                    s1.at[b, j, d],
                    r1.at[b, j, d],
                    s,
                    other,
                )
            )

    def gather_wait(b, j):
        for d, other in enumerate(froms):
            theirs = tables.at[b, part(other), pl.ds(REACH + j * REACH, REACH)]
            remote(theirs, theirs, s1.at[b, j, d], r1.at[b, j, d], s, other).wait_recv()

    def places_along_z():
        for d in range(1, side):
            other = (lax.rem(zz + d, side) * side + yy) * 2 + core
            ship(remote(place, places.at[zz, yy, core], s6.at[d - 1], r6.at[d - 1], other, h))

    def places_along_y():
        loads[6].wait()
        for d in range(1, side):
            theirs = places.at[lax.rem(zz + side - d, side), yy, core]
            remote(theirs, theirs, s6.at[d - 1], r6.at[d - 1], s, h).wait_recv()
        for d in range(1, side):
            other = (zz * side + lax.rem(yy + d, side)) * 2 + core
            column = places.at[:, yy, core]
            ship(remote(column, column, s7.at[d - 1], r7.at[d - 1], other, h))

    def places_across():
        for d in range(1, side):
            theirs = places.at[:, lax.rem(yy + side - d, side), core]
            remote(theirs, theirs, s7.at[d - 1], r7.at[d - 1], s, h).wait_recv()
        column = places.at[:, :, core]
        ship(remote(column, column, s8.at[0], r8.at[0], sibling, h))

    def places_finish():
        theirs = places.at[:, :, 1 - core]
        remote(theirs, theirs, s8.at[0], r8.at[0], sibling, h).wait_recv()
        for line in range(lines):
            pltpu.make_async_copy(
                places.at[:, :, line // (lines // 2), line % (lines // 2)], pv.at[line], local.at[7]
            ).start()

    def weights_start():
        loads[5].wait()
        both = jnp.concatenate([p[0], p[1]], axis=0).astype(F32)
        pq[...] = both.T.astype(BF16)
        for d, other in enumerate(peers):
            ship(remote(pq.at[part(other), :], pall.at[h], s5.at[d], r5.at[d], s, other))
        pall[h] = pq[mine, :]

    def weights_finish():
        for d, other in enumerate(froms):
            remote(pall.at[other], pall.at[other], s5.at[d], r5.at[d], s, other).wait_recv()
        for b in range(2):
            span = slice(b * width, (b + 1) * width)
            pt[b] = jnp.concatenate([pall[g, :, span].astype(F32) for g in range(groups)], axis=1).astype(BF16)

    batch = 16
    strip = batch * CAP
    strips = chips // batch

    def prepare():
        weights_finish()
        places_finish()
        column = lax.broadcasted_iota(jnp.int32, (chips, LANES), 0)
        run = jnp.zeros((chips, 1), F32)
        half = lines // 2
        slots = []
        for line in range(lines):
            row = places[zz, yy, line // half, line % half : line % half + 1, :]
            device = row >> bits
            mask = jnp.where(device == column * 2 + core, 1.0, 0.0)
            counts = jnp.dot(mask.astype(BF16), tri[...], preferred_element_type=F32) + run
            run = counts[:, LANES - 1 :]
            rank = (jnp.sum(mask * counts, axis=0, keepdims=True) - 1.0).astype(jnp.int32)
            here = (device & 1) == core
            target = (device >> 1) * CAP + (rank & (CAP - 1))
            slots.append((jnp.where(here, target, -1), rank >> 4))
        spot = lax.broadcasted_iota(jnp.int32, (strip, rows), 0)
        for c in range(2):
            targets = jnp.concatenate([t for t, _ in slots[c * half : (c + 1) * half]], axis=1)
            halves = jnp.concatenate([e for _, e in slots[c * half : (c + 1) * half]], axis=1)
            side_of[c : c + 1, :] = halves
            for i in range(strips):
                rows_of = slice(i * strip, (i + 1) * strip)
                onehot[c, rows_of, :] = (spot == targets - i * strip).astype(F32).astype(BF16)

    def run_block(b):
        table = tables.at[b]
        mix = mixes.at[b]
        ho = heads_out.at[b]
        gather_wait(b, 0)
        first = remote(
            table.at[:, pl.ds(REACH, REACH)],
            table.at[:, pl.ds(REACH + rows, REACH)],
            s2.at[b, 0],
            r2.at[b, 0],
            before,
            h,
        )
        ship(first)
        if b == 0:
            places_along_y()
            for load in loads[1:5]:
                load.wait()
        taps = w[b].reshape(TAPS * width, -1)

        def products(tile):
            points = table[:, tile * REACH : (tile + 1) * REACH]
            value = jnp.dot(taps, points, preferred_element_type=F32).astype(BF16)
            y[:, tile] = value.reshape(TAPS, width, REACH)

        def conv(blk):
            cols = slice(blk * REACH, (blk + 1) * REACH)
            base = s * rows + (blk - 1) * REACH
            total = jnp.zeros((width, REACH), F32)
            for t in range(TAPS):
                index = nb[t, b : b + 1, cols]
                spot = index - base
                tile = jnp.where(index < 0, 3, spot >> 8)
                within = (spot & (REACH - 1)).astype(F32).astype(BF16)
                chosen = jnp.where(position == within, one, zero)
                terms = y[t, blk : blk + 3].reshape(3 * width, REACH)
                picked = jnp.dot(terms, chosen, preferred_element_type=F32)
                term = jnp.where(tile == 0, picked[:width], 0.0)
                term = jnp.where(tile == 1, picked[width : 2 * width], term)
                term = jnp.where(tile == 2, picked[2 * width :], term)
                total = total + term
            own = table[mine, REACH + blk * REACH : REACH + (blk + 1) * REACH].astype(F32)
            mix[mine, cols] = (own + total).astype(BF16)
            for d, other in enumerate(peers):
                ship(remote(mix.at[mine, cols], mix.at[mine, cols], s3.at[b, blk, d], r3.at[b, blk, d], s, other))

        products(1)
        for tile in range(2, blocks):
            gather_wait(b, tile - 1)
            products(tile)
        conv(1)
        gather_wait(b, blocks - 1)
        last = remote(
            table.at[:, pl.ds(rows, REACH)],
            table.at[:, pl.ds(0, REACH)],
            s2.at[b, 1],
            r2.at[b, 1],
            after,
            h,
        )
        ship(last)
        products(blocks)
        for blk in range(2, blocks - 1):
            conv(blk)
        if b == 0:
            places_across()
        first.wait_recv()
        products(blocks + 1)
        conv(blocks - 1)
        last.wait_recv()
        products(0)
        conv(0)
        if b == 0:
            prepare()

        scale = 1.0 / HD**0.5
        bias = jnp.where(vm[b : b + 1, :] > 0, 0.0, -1e30)
        weights = a[b].reshape(3 * width, -1)
        for blk in (*range(1, blocks), 0):
            cols = slice(blk * REACH, (blk + 1) * REACH)
            for d, other in enumerate(froms):
                theirs = mix.at[part(other), cols]
                remote(theirs, theirs, s3.at[b, blk, d], r3.at[b, blk, d], s, other).wait_recv()
            values = mix[:, cols].astype(F32)
            centred = values - jnp.mean(values, axis=0, keepdims=True)
            variance = jnp.mean(centred * centred, axis=0, keepdims=True)
            normed = (centred * lax.rsqrt(variance + 1e-05)).astype(BF16)
            qkv = jnp.dot(weights, normed, preferred_element_type=F32)
            query = (qkv[:width].astype(BF16).astype(F32) * scale).astype(BF16)
            value = qkv[2 * width :].astype(BF16)
            for hd in range(heads):
                span = slice(hd * HD, (hd + 1) * HD)
                qm[hd, span, cols] = query[span]
                va[hd, :HD, cols] = value[span]
            tail = jnp.where(
                lax.broadcasted_iota(jnp.int32, (width, REACH), 0) == 0, bias[:, cols], 0.0
            )
            keys = jnp.concatenate([qkv[width : 2 * width], tail], axis=0)
            kt[cols, :] = keys.T.astype(BF16)

        def score(hd):
            return jnp.dot(kt[...], qm[hd], preferred_element_type=F32)

        upcoming = score(0)
        for hd in range(heads):
            scores = upcoming
            if hd + 1 < heads:
                upcoming = score(hd + 1)
            top = jnp.max(scores, axis=0, keepdims=True)
            probs = jnp.exp(scores - top).astype(BF16)
            summed = jnp.dot(va[hd], probs, preferred_element_type=F32)
            result = summed[:HD] / summed[HD : HD + 1]
            span = part(h, HD, hd * HD)
            ho[span, :] = result.astype(BF16)
            for d, other in enumerate(peers):
                ship(remote(ho.at[span, :], ho.at[span, :], s4.at[b, hd, d], r4.at[b, hd, d], s, other))

    def project(b):
        mix = mixes.at[b]
        ho = heads_out.at[b]
        for hd in range(heads):
            for d, other in enumerate(froms):
                theirs = ho.at[part(other, HD, hd * HD), :]
                remote(theirs, theirs, s4.at[b, hd, d], r4.at[b, hd, d], s, other).wait_recv()
        update = jnp.dot(pt[b], ho[...], preferred_element_type=F32)
        return (mix[mine, :].astype(F32) + update).astype(BF16)

    for j in range(blocks):
        gather_piece(0, x, j)
    places_along_z()
    low = lax.broadcasted_iota(jnp.int32, (LANES, LANES), 0)
    high = lax.broadcasted_iota(jnp.int32, (LANES, LANES), 1)
    tri[...] = jnp.where(low <= high, 1.0, 0.0).astype(BF16)
    position = lax.broadcasted_iota(jnp.int32, (REACH, REACH), 0).astype(F32).astype(BF16)
    one, zero = jnp.ones((), BF16), jnp.zeros((), BF16)
    ones = jnp.where(lax.broadcasted_iota(jnp.int32, (HD, rows), 0) == 0, 1.0, 0.0).astype(BF16)
    qm[...] = jnp.zeros(qm.shape, BF16)
    for hd in range(heads):
        qm[hd, width : width + HD, :] = ones
        va[hd, HD:, :] = ones
    weights_start()
    loads[0].wait()
    run_block(0)

    feats[core] = project(0)
    swap = remote(feats.at[core], feats.at[core], s9.at[0], r9.at[0], sibling, h)
    ship(swap)
    own = chip // batch

    def turn_points(c):
        points = feats[c].astype(F32)
        half_of = side_of[pl.ds(c, 1), :]
        both = jnp.concatenate([jnp.where(half_of == e, points, 0.0) for e in range(2)], axis=0)
        turned_feats[c] = both.T.astype(BF16)

    def sorted_part(c, which):
        span = pl.ds(pl.multiple_of(which * strip, strip), strip)
        return span, jnp.dot(onehot[c, span, :], turned_feats[c], preferred_element_type=F32)

    def sort_own(which, carry):
        span, value = sorted_part(core, which)
        partial[span, :] = value
        return carry

    turn_points(core)
    lax.fori_loop(0, strips, sort_own, 0, unroll=2)
    theirs = feats.at[1 - core]
    remote(theirs, theirs, s9.at[0], r9.at[0], sibling, h).wait_recv()
    turn_points(1 - core)

    def sort(i, carry):
        which = lax.rem(own + i, strips)
        span, value = sorted_part(1 - core, which)
        both = (partial[span, :] + value).astype(BF16)
        going[pl.ds(which * batch, batch)] = both.reshape(batch, CAP, 2 * width)

        def send(j, c):
            other = which * batch + lax.rem(chip + j, batch)

            @pl.when(other != chip)
            def _():
                remote(going.at[other], come.at[chip], s10.at[0], r10.at[0], other * 2 + core, h).start()

            return c

        lax.fori_loop(0, batch, send, 0)
        return carry

    lax.fori_loop(0, strips, sort, 0)
    stay = pltpu.make_async_copy(going.at[chip], come.at[chip], local.at[8])
    stay.start()

    pltpu.make_async_copy(pv, pv, local.at[7]).wait()
    run = jnp.zeros((chips, 1), F32)
    for line in range(lines):
        row = pv[line].reshape(chips, LANES)
        mask = jnp.where((row >> bits) == s, 1.0, 0.0)
        counts = jnp.dot(mask.astype(BF16), tri[...], preferred_element_type=F32) + run
        run = counts[:, LANES - 1 :]
        land[line] = jnp.where(mask > 0, counts - 1.0, -1.0)
        flat[line] = ((row & (rows - 1)) + 1).astype(F32)
    for start in range(0, chips, 8):
        ranks = [land[line, start : start + 8, :] for line in range(lines)]
        spots = [flat[line, start : start + 8, :] for line in range(lines)]

        def settle(k, carry):
            rank = k.astype(F32)
            total = jnp.zeros((8, LANES), F32)
            for line in range(lines):
                total += jnp.where(ranks[line] == rank, spots[line], 0.0)
            where = jnp.sum(total, axis=1, keepdims=True)
            found[pl.ds(pl.multiple_of(k * chips + start, 8), 8), :] = jnp.broadcast_to(where, (8, LANES))
            return carry

        lax.fori_loop(0, 2 * CAP, settle, 0, unroll=8)
    lane = lax.broadcasted_iota(jnp.int32, (chips, LANES), 1).astype(F32) + 1.0

    def turn(k, carry):
        span = pl.ds(pl.multiple_of(k * chips, 16), chips)
        spots = found[span, :]
        for start in range(0, rows, LANES):
            turned[span, start : start + LANES] = (spots == lane + float(start)).astype(F32).astype(BF16)
        return carry

    lax.fori_loop(0, 2 * CAP, turn, 0, unroll=2)

    stay.wait()
    many = pl.ds(0, chips - 1)
    every = remote(going.at[many], come.at[many], s10.at[0], r10.at[0], sibling, h)
    every.wait_recv()
    arrived = come[...].astype(F32)
    parts = []
    for k in range(0, CAP, 2):
        two = jnp.concatenate([arrived[:, k, :], arrived[:, k + 1, :]], axis=0)
        parts.append(two.T.astype(BF16))
    packed = jnp.concatenate(parts, axis=1)
    half = CAP * chips
    for j in range(blocks):
        cols = slice(j * REACH, (j + 1) * REACH)
        total = jnp.dot(packed[:width], turned[:half, cols], preferred_element_type=F32)
        total += jnp.dot(packed[width:], turned[half:, cols], preferred_element_type=F32)
        moved[:, cols] = total.astype(BF16)
        gather_piece(1, moved, j)
    tables[1, mine, REACH : REACH + rows] = moved[...]
    run_block(1)
    out[...] = project(1)
    for copy in sends:
        copy.wait_send()
    every.wait_send()


def body(groups, side, features, neighbours, valid, conv_weight, attn_weight, proj_weight, hilbert_place):
    width, rows = features.shape
    channels = width * groups
    heads = width // HD
    blocks = rows // REACH
    chips = side * side
    lines = 2 * rows // LANES
    others = groups - 1
    dma = pltpu.SemaphoreType.DMA
    vmem = pltpu.VMEM
    pairs = [(2, blocks, others), (2, 2), (2, blocks, others), (2, heads, others), (others,)]
    pairs += [(side - 1,), (side - 1,), (1,), (1,), (1,)]
    return pl.pallas_call(
        kernel,
        out_shape=jax.ShapeDtypeStruct((width, rows), BF16),
        in_specs=[pl.BlockSpec(memory_space=pl.ANY)] * 7,
        out_specs=pl.BlockSpec(memory_space=pltpu.VMEM),
        scratch_shapes=[
            vmem((2, channels, rows + 2 * REACH), BF16),
            vmem((2, channels, rows), BF16),
            vmem((2, channels, rows), BF16),
            vmem((TAPS, 2, rows), jnp.int32),
            vmem((2, rows), jnp.int32),
            vmem((2, TAPS, width, channels), BF16),
            vmem((2, 3, width, channels), BF16),
            vmem((2, width, channels), BF16),
            vmem((channels, 2 * width), BF16),
            vmem((groups, width, 2 * width), BF16),
            vmem((2, width, channels), BF16),
            vmem((TAPS, blocks + 2, width, REACH), BF16),
            vmem((rows, 2 * width), BF16),
            vmem((heads, 2 * width, rows), BF16),
            vmem((heads, 2 * HD, rows), BF16),
            vmem((side, side, 2, rows // LANES, LANES), jnp.int32),
            vmem((lines, side, side, LANES), jnp.int32),
            vmem((2, width, rows), BF16),
            vmem((LANES, LANES), BF16),
            vmem((2, chips * CAP, rows), BF16),
            vmem((2, rows), jnp.int32),
            vmem((2, rows, 2 * width), BF16),
            vmem((chips * CAP, 2 * width), F32),
            vmem((chips, CAP, 2 * width), BF16),
            vmem((chips, CAP, 2 * width), BF16),
            vmem((lines, chips, LANES), F32),
            vmem((lines, chips, LANES), F32),
            vmem((2 * CAP * chips, LANES), F32),
            vmem((2 * CAP * chips, rows), BF16),
            vmem((width, rows), BF16),
            dma((9,)),
            *[dma(shape) for shape in pairs for _ in range(2)],
        ],
        compiler_params=pltpu.CompilerParams(
            collective_id=0, has_side_effects=True, vmem_limit_bytes=60 * 2**20
        ),
        name="blocks",
    )(
        features,
        jnp.swapaxes(neighbours, 0, 1),
        valid,
        conv_weight,
        attn_weight,
        proj_weight,
        hilbert_place.reshape(rows // LANES, LANES),
    )


def solution(mesh):
    in_specs = (
        P("head", "seq"),
        P(None, None, "seq"),
        P(None, "seq"),
        P(None, None, "head", None),
        P(None, None, "head", None),
        P(None, "head", None),
        P("seq"),
    )
    return jax.shard_map(
        functools.partial(body, mesh.shape["head"], math.isqrt(mesh.shape["seq"] // 2)),
        mesh=mesh,
        in_specs=in_specs,
        out_specs=P("head", "seq"),
        check_vma=False,
    )
```

```python
import functools
import math

import jax
import jax.numpy as jnp
from jax import lax
from jax.experimental import pallas as pl
from jax.experimental.pallas import tpu as pltpu
from jax.sharding import PartitionSpec as P

HD = 16
REACH = 256
TAPS = 27
CAP = 16
LANES = 128
MESH = pl.DeviceIdType.MESH
BF16 = jnp.bfloat16
F32 = jnp.float32


def remote(src, dst, send, recv, s, h):
    return pltpu.make_async_remote_copy(
        src_ref=src,
        dst_ref=dst,
        send_sem=send,
        recv_sem=recv,
        device_id=(s, h),
        device_id_type=MESH,
    )


def kernel(
    x,
    nbr,
    valid,
    cw,
    aw,
    pw,
    place,
    heads_last,
    mix_out,
    weight_out,
    tables,
    mixes,
    heads_first,
    nb,
    vm,
    w,
    a,
    p,
    pq,
    pall,
    pt,
    y,
    kt,
    qm,
    va,
    places,
    pv,
    feats,
    tri,
    onehot,
    side_of,
    turned_feats,
    partial,
    going,
    come,
    land,
    flat,
    found,
    turned,
    moved,
    local,
    s1,
    r1,
    s2,
    r2,
    s3,
    r3,
    s4,
    r4,
    s5,
    r5,
    s6,
    r6,
    s7,
    r7,
    s8,
    r8,
    s9,
    r9,
    s10,
    r10,
):
    width, rows = mix_out.shape
    heads = width // HD
    heads_out = (heads_first, heads_last)
    steps = [(0, 0, rows // 2), (0, rows // 2, rows // 2)] + [(hd, 0, rows) for hd in range(1, heads)]
    groups = lax.axis_size("head")
    shards = lax.axis_size("seq")
    side = places.shape[0]
    chips = side * side
    lines = 2 * places.shape[3]
    blocks = rows // REACH
    bits = rows.bit_length() - 1
    s = lax.axis_index("seq")
    h = lax.axis_index("head")
    core = lax.rem(s, 2)
    chip = s // 2
    zz = chip // side
    yy = lax.rem(chip, side)
    sibling = s + 1 - 2 * core
    after = lax.rem(s + 1, shards)
    before = lax.rem(s + shards - 1, shards)
    peers = [lax.rem(h + d, groups) for d in range(1, groups)]
    froms = [lax.rem(h + groups - d, groups) for d in range(1, groups)]
    sends = []

    def part(index, size=width, extra=0):
        return pl.ds(pl.multiple_of(index * width + extra, 16), size)

    mine = part(h)

    def ship(copy):
        copy.start()
        sends.append(copy)

    barrier = pltpu.get_barrier_semaphore()

    def greet(i, carry):
        other = lax.rem(chip + i, chips) * 2 + core
        pl.semaphore_signal(barrier, inc=1, device_id=(other, h), device_id_type=MESH)
        return carry

    for other in peers:
        pl.semaphore_signal(barrier, inc=1, device_id=(s, other), device_id_type=MESH)
    for other in (before, after):
        pl.semaphore_signal(barrier, inc=1, device_id=(other, h), device_id_type=MESH)
    lax.fori_loop(1, chips, greet, 0)
    loads = [
        pltpu.make_async_copy(x, tables.at[0, mine, pl.ds(REACH, rows)], local.at[0]),
        pltpu.make_async_copy(cw, w, local.at[1]),
        pltpu.make_async_copy(nbr, nb, local.at[2]),
        pltpu.make_async_copy(valid, vm, local.at[3]),
        pltpu.make_async_copy(aw, a, local.at[4]),
        pltpu.make_async_copy(pw, p, local.at[5]),
        pltpu.make_async_copy(place, places.at[zz, yy, core], local.at[6]),
    ]
    for load in loads:
        load.start()
    pl.semaphore_wait(barrier, chips - 1 + groups - 1 + 2)

    def gather_piece(b, source, j):
        for d, other in enumerate(peers):
            span = pl.ds(REACH + j * REACH, REACH)
            ship(
                remote(
                    source.at[:, pl.ds(j * REACH, REACH)],
                    tables.at[b, mine, span],
                    s1.at[b, j, d],
                    r1.at[b, j, d],
                    s,
                    other,
                )
            )

    def gather_wait(b, j):
        for d, other in enumerate(froms):
            theirs = tables.at[b, part(other), pl.ds(REACH + j * REACH, REACH)]
            remote(theirs, theirs, s1.at[b, j, d], r1.at[b, j, d], s, other).wait_recv()

    def places_along_z():
        for d in range(1, side):
            other = (lax.rem(zz + d, side) * side + yy) * 2 + core
            ship(remote(place, places.at[zz, yy, core], s6.at[d - 1], r6.at[d - 1], other, h))

    def places_along_y():
        loads[6].wait()
        for d in range(1, side):
            theirs = places.at[lax.rem(zz + side - d, side), yy, core]
            remote(theirs, theirs, s6.at[d - 1], r6.at[d - 1], s, h).wait_recv()
        for d in range(1, side):
            other = (zz * side + lax.rem(yy + d, side)) * 2 + core
            column = places.at[:, yy, core]
            ship(remote(column, column, s7.at[d - 1], r7.at[d - 1], other, h))

    def places_across():
        for d in range(1, side):
            theirs = places.at[:, lax.rem(yy + side - d, side), core]
            remote(theirs, theirs, s7.at[d - 1], r7.at[d - 1], s, h).wait_recv()
        column = places.at[:, :, core]
        ship(remote(column, column, s8.at[0], r8.at[0], sibling, h))

    def places_finish():
        theirs = places.at[:, :, 1 - core]
        remote(theirs, theirs, s8.at[0], r8.at[0], sibling, h).wait_recv()
        for line in range(lines):
            pltpu.make_async_copy(
                places.at[:, :, line // (lines // 2), line % (lines // 2)], pv.at[line], local.at[7]
            ).start()

    def weights_start():
        loads[5].wait()
        both = jnp.concatenate([p[0], p[1]], axis=0).astype(F32)
        pq[...] = both.T.astype(BF16)
        for d, other in enumerate(peers):
            ship(remote(pq.at[part(other), :], pall.at[h], s5.at[d], r5.at[d], s, other))
        pall[h] = pq[mine, :]

    def weights_finish():
        for d, other in enumerate(froms):
            remote(pall.at[other], pall.at[other], s5.at[d], r5.at[d], s, other).wait_recv()
        for b in range(2):
            span = slice(b * width, (b + 1) * width)
            pt[b] = jnp.concatenate([pall[g, :, span].astype(F32) for g in range(groups)], axis=1).astype(BF16)

    batch = 16
    strip = batch * CAP
    strips = chips // batch

    def prepare():
        weights_finish()
        places_finish()
        column = lax.broadcasted_iota(jnp.int32, (chips, LANES), 0)
        run = jnp.zeros((chips, 1), F32)
        half = lines // 2
        slots = []
        for line in range(lines):
            row = places[zz, yy, line // half, line % half : line % half + 1, :]
            device = row >> bits
            mask = jnp.where(device == column * 2 + core, 1.0, 0.0)
            counts = jnp.dot(mask.astype(BF16), tri[...], preferred_element_type=F32) + run
            run = counts[:, LANES - 1 :]
            rank = (jnp.sum(mask * counts, axis=0, keepdims=True) - 1.0).astype(jnp.int32)
            here = (device & 1) == core
            target = (device >> 1) * CAP + (rank & (CAP - 1))
            slots.append((jnp.where(here, target, -1), rank >> 4))
        spot = lax.broadcasted_iota(jnp.int32, (strip, rows), 0)
        for c in range(2):
            targets = jnp.concatenate([t for t, _ in slots[c * half : (c + 1) * half]], axis=1)
            halves = jnp.concatenate([e for _, e in slots[c * half : (c + 1) * half]], axis=1)
            side_of[c : c + 1, :] = halves
            for i in range(strips):
                rows_of = slice(i * strip, (i + 1) * strip)
                onehot[c, rows_of, :] = (spot == targets - i * strip).astype(F32).astype(BF16)

    def run_block(b):
        table = tables.at[b]
        mix = mixes.at[b]
        ho = heads_out[b]
        gather_wait(b, 0)
        first = remote(
            table.at[:, pl.ds(REACH, REACH)],
            table.at[:, pl.ds(REACH + rows, REACH)],
            s2.at[b, 0],
            r2.at[b, 0],
            before,
            h,
        )
        ship(first)
        if b == 0:
            places_along_y()
            for load in loads[1:5]:
                load.wait()
        taps = w[b].reshape(TAPS * width, -1)

        def products(tile):
            points = table[:, tile * REACH : (tile + 1) * REACH]
            value = jnp.dot(taps, points, preferred_element_type=F32).astype(BF16)
            y[:, tile] = value.reshape(TAPS, width, REACH)

        def conv(blk):
            cols = slice(blk * REACH, (blk + 1) * REACH)
            base = s * rows + (blk - 1) * REACH
            total = jnp.zeros((width, REACH), F32)
            for t in range(TAPS):
                index = nb[t, b : b + 1, cols]
                spot = index - base
                tile = jnp.where(index < 0, 3, spot >> 8)
                within = (spot & (REACH - 1)).astype(F32).astype(BF16)
                chosen = jnp.where(position == within, one, zero)
                terms = y[t, blk : blk + 3].reshape(3 * width, REACH)
                picked = jnp.dot(terms, chosen, preferred_element_type=F32)
                term = jnp.where(tile == 0, picked[:width], 0.0)
                term = jnp.where(tile == 1, picked[width : 2 * width], term)
                term = jnp.where(tile == 2, picked[2 * width :], term)
                total = total + term
            own = table[mine, REACH + blk * REACH : REACH + (blk + 1) * REACH].astype(F32)
            mix[mine, cols] = (own + total).astype(BF16)
            for d, other in enumerate(peers):
                ship(remote(mix.at[mine, cols], mix.at[mine, cols], s3.at[b, blk, d], r3.at[b, blk, d], s, other))

        products(1)
        for tile in range(2, blocks):
            gather_wait(b, tile - 1)
            products(tile)
        conv(1)
        gather_wait(b, blocks - 1)
        last = remote(
            table.at[:, pl.ds(rows, REACH)],
            table.at[:, pl.ds(0, REACH)],
            s2.at[b, 1],
            r2.at[b, 1],
            after,
            h,
        )
        ship(last)
        products(blocks)
        for blk in range(2, blocks - 1):
            conv(blk)
        if b == 0:
            places_across()
        first.wait_recv()
        products(blocks + 1)
        conv(blocks - 1)
        last.wait_recv()
        products(0)
        conv(0)

        scale = 1.0 / HD**0.5
        bias = jnp.where(vm[b : b + 1, :] > 0, 0.0, -1e30)
        weights = a[b].reshape(3 * width, -1)
        for blk in (*range(1, blocks), 0):
            cols = slice(blk * REACH, (blk + 1) * REACH)
            for d, other in enumerate(froms):
                theirs = mix.at[part(other), cols]
                remote(theirs, theirs, s3.at[b, blk, d], r3.at[b, blk, d], s, other).wait_recv()
            values = mix[:, cols].astype(F32)
            centred = values - jnp.mean(values, axis=0, keepdims=True)
            variance = jnp.mean(centred * centred, axis=0, keepdims=True)
            normed = (centred * lax.rsqrt(variance + 1e-05)).astype(BF16)
            qkv = jnp.dot(weights, normed, preferred_element_type=F32)
            query = (qkv[:width].astype(BF16).astype(F32) * scale).astype(BF16)
            value = qkv[2 * width :].astype(BF16)
            for hd in range(heads):
                span = slice(hd * HD, (hd + 1) * HD)
                qm[hd, span, cols] = query[span]
                va[hd, :HD, cols] = value[span]
            tail = jnp.where(
                lax.broadcasted_iota(jnp.int32, (width, REACH), 0) == 0, bias[:, cols], 0.0
            )
            keys = jnp.concatenate([qkv[width : 2 * width], tail], axis=0)
            kt[cols, :] = keys.T.astype(BF16)

        def score(i):
            hd, low, size = steps[i]
            return jnp.dot(kt[...], qm[hd, :, low : low + size], preferred_element_type=F32)

        upcoming = score(0)
        for i, (hd, low, size) in enumerate(steps):
            scores = upcoming
            if i + 1 < len(steps):
                upcoming = score(i + 1)
            top = jnp.max(scores, axis=0, keepdims=True)
            probs = jnp.exp(scores - top).astype(BF16)
            summed = jnp.dot(va[hd], probs, preferred_element_type=F32)
            result = summed[:HD] / summed[HD : HD + 1]
            span = part(h, HD, hd * HD)
            ho[span, low : low + size] = result.astype(BF16)
            for d, other in enumerate(peers):
                piece = ho.at[span, pl.ds(low, size)]
                ship(remote(piece, piece, s4.at[b, i, d], r4.at[b, i, d], s, other))

    def heads_wait(b):
        for i, (hd, low, size) in enumerate(steps):
            for d, other in enumerate(froms):
                theirs = heads_out[b].at[part(other, HD, hd * HD), pl.ds(low, size)]
                remote(theirs, theirs, s4.at[b, i, d], r4.at[b, i, d], s, other).wait_recv()

    for j in range(blocks):
        gather_piece(0, x, j)
    places_along_z()
    low = lax.broadcasted_iota(jnp.int32, (LANES, LANES), 0)
    high = lax.broadcasted_iota(jnp.int32, (LANES, LANES), 1)
    tri[...] = jnp.where(low <= high, 1.0, 0.0).astype(BF16)
    position = lax.broadcasted_iota(jnp.int32, (REACH, REACH), 0).astype(F32).astype(BF16)
    one, zero = jnp.ones((), BF16), jnp.zeros((), BF16)
    ones = jnp.where(lax.broadcasted_iota(jnp.int32, (HD, rows), 0) == 0, 1.0, 0.0).astype(BF16)
    qm[...] = jnp.zeros(qm.shape, BF16)
    for hd in range(heads):
        qm[hd, width : width + HD, :] = ones
        va[hd, HD:, :] = ones
    weights_start()
    loads[0].wait()
    run_block(0)
    prepare()

    heads_wait(0)
    update = jnp.dot(pt[0], heads_out[0][...], preferred_element_type=F32)
    feats[core] = (mixes[0, mine, :].astype(F32) + update).astype(BF16)
    swap = remote(feats.at[core], feats.at[core], s9.at[0], r9.at[0], sibling, h)
    ship(swap)
    own = chip // batch

    def turn_points(c):
        points = feats[c].astype(F32)
        half_of = side_of[pl.ds(c, 1), :]
        both = jnp.concatenate([jnp.where(half_of == e, points, 0.0) for e in range(2)], axis=0)
        turned_feats[c] = both.T.astype(BF16)

    def sorted_part(c, which):
        span = pl.ds(pl.multiple_of(which * strip, strip), strip)
        return span, jnp.dot(onehot[c, span, :], turned_feats[c], preferred_element_type=F32)

    def sort_own(which, carry):
        span, value = sorted_part(core, which)
        partial[span, :] = value
        return carry

    turn_points(core)
    lax.fori_loop(0, strips, sort_own, 0, unroll=2)
    theirs = feats.at[1 - core]
    remote(theirs, theirs, s9.at[0], r9.at[0], sibling, h).wait_recv()
    turn_points(1 - core)

    def sort(i, carry):
        which = lax.rem(own + i, strips)
        span, value = sorted_part(1 - core, which)
        both = (partial[span, :] + value).astype(BF16)
        going[pl.ds(which * batch, batch)] = both.reshape(batch, CAP, 2 * width)

        def send(j, c):
            other = which * batch + lax.rem(chip + j, batch)

            @pl.when(other != chip)
            def _():
                remote(going.at[other], come.at[chip], s10.at[0], r10.at[0], other * 2 + core, h).start()

            return c

        lax.fori_loop(0, batch, send, 0)
        return carry

    lax.fori_loop(0, strips, sort, 0)
    stay = pltpu.make_async_copy(going.at[chip], come.at[chip], local.at[8])
    stay.start()

    pltpu.make_async_copy(pv, pv, local.at[7]).wait()
    run = jnp.zeros((chips, 1), F32)
    for line in range(lines):
        row = pv[line].reshape(chips, LANES)
        mask = jnp.where((row >> bits) == s, 1.0, 0.0)
        counts = jnp.dot(mask.astype(BF16), tri[...], preferred_element_type=F32) + run
        run = counts[:, LANES - 1 :]
        land[line] = jnp.where(mask > 0, counts - 1.0, -1.0)
        flat[line] = ((row & (rows - 1)) + 1).astype(F32)
    for start in range(0, chips, 8):
        ranks = [land[line, start : start + 8, :] for line in range(lines)]
        spots = [flat[line, start : start + 8, :] for line in range(lines)]

        def settle(k, carry):
            rank = k.astype(F32)
            total = jnp.zeros((8, LANES), F32)
            for line in range(lines):
                total += jnp.where(ranks[line] == rank, spots[line], 0.0)
            where = jnp.sum(total, axis=1, keepdims=True)
            found[pl.ds(pl.multiple_of(k * chips + start, 8), 8), :] = jnp.broadcast_to(where, (8, LANES))
            return carry

        lax.fori_loop(0, 2 * CAP, settle, 0, unroll=8)
    lane = lax.broadcasted_iota(jnp.int32, (chips, LANES), 1).astype(F32) + 1.0

    def turn(k, carry):
        span = pl.ds(pl.multiple_of(k * chips, 16), chips)
        spots = found[span, :]
        for start in range(0, rows, LANES):
            turned[span, start : start + LANES] = (spots == lane + float(start)).astype(F32).astype(BF16)
        return carry

    lax.fori_loop(0, 2 * CAP, turn, 0, unroll=2)

    stay.wait()
    many = pl.ds(0, chips - 1)
    every = remote(going.at[many], come.at[many], s10.at[0], r10.at[0], sibling, h)
    every.wait_recv()
    arrived = come[...].astype(F32)
    parts = []
    for k in range(0, CAP, 2):
        two = jnp.concatenate([arrived[:, k, :], arrived[:, k + 1, :]], axis=0)
        parts.append(two.T.astype(BF16))
    packed = jnp.concatenate(parts, axis=1)
    half = CAP * chips
    for j in range(blocks):
        cols = slice(j * REACH, (j + 1) * REACH)
        total = jnp.dot(packed[:width], turned[:half, cols], preferred_element_type=F32)
        total += jnp.dot(packed[width:], turned[half:, cols], preferred_element_type=F32)
        moved[:, cols] = total.astype(BF16)
        gather_piece(1, moved, j)
    tables[1, mine, REACH : REACH + rows] = moved[...]
    run_block(1)
    mix_out[...] = mixes[1, mine, :]
    weight_out[...] = pt[1]
    heads_wait(1)
    for copy in sends:
        copy.wait_send()
    every.wait_send()


def body(groups, side, features, neighbours, valid, conv_weight, attn_weight, proj_weight, hilbert_place):
    width, rows = features.shape
    channels = width * groups
    heads = width // HD
    blocks = rows // REACH
    chips = side * side
    lines = 2 * rows // LANES
    others = groups - 1
    dma = pltpu.SemaphoreType.DMA
    vmem = pltpu.VMEM
    pairs = [(2, blocks, others), (2, 2), (2, blocks, others), (2, heads + 1, others), (others,)]
    pairs += [(side - 1,), (side - 1,), (1,), (1,), (1,)]
    heads_all, mixed, weight = pl.pallas_call(
        kernel,
        out_shape=[
            jax.ShapeDtypeStruct((channels, rows), BF16),
            jax.ShapeDtypeStruct((width, rows), BF16),
            jax.ShapeDtypeStruct((width, channels), BF16),
        ],
        in_specs=[pl.BlockSpec(memory_space=pl.ANY)] * 7,
        out_specs=[pl.BlockSpec(memory_space=pltpu.VMEM)] * 3,
        scratch_shapes=[
            vmem((2, channels, rows + 2 * REACH), BF16),
            vmem((2, channels, rows), BF16),
            vmem((channels, rows), BF16),
            vmem((TAPS, 2, rows), jnp.int32),
            vmem((2, rows), jnp.int32),
            vmem((2, TAPS, width, channels), BF16),
            vmem((2, 3, width, channels), BF16),
            vmem((2, width, channels), BF16),
            vmem((channels, 2 * width), BF16),
            vmem((groups, width, 2 * width), BF16),
            vmem((2, width, channels), BF16),
            vmem((TAPS, blocks + 2, width, REACH), BF16),
            vmem((rows, 2 * width), BF16),
            vmem((heads, 2 * width, rows), BF16),
            vmem((heads, 2 * HD, rows), BF16),
            vmem((side, side, 2, rows // LANES, LANES), jnp.int32),
            vmem((lines, side, side, LANES), jnp.int32),
            vmem((2, width, rows), BF16),
            vmem((LANES, LANES), BF16),
            vmem((2, chips * CAP, rows), BF16),
            vmem((2, rows), jnp.int32),
            vmem((2, rows, 2 * width), BF16),
            vmem((chips * CAP, 2 * width), F32),
            vmem((chips, CAP, 2 * width), BF16),
            vmem((chips, CAP, 2 * width), BF16),
            vmem((lines, chips, LANES), F32),
            vmem((lines, chips, LANES), F32),
            vmem((2 * CAP * chips, LANES), F32),
            vmem((2 * CAP * chips, rows), BF16),
            vmem((width, rows), BF16),
            dma((9,)),
            *[dma(shape) for shape in pairs for _ in range(2)],
        ],
        compiler_params=pltpu.CompilerParams(
            collective_id=0, has_side_effects=True, vmem_limit_bytes=60 * 2**20
        ),
        name="blocks",
    )(
        features,
        jnp.swapaxes(neighbours, 0, 1),
        valid,
        conv_weight,
        attn_weight,
        proj_weight,
        hilbert_place.reshape(rows // LANES, LANES),
    )
    update = jnp.dot(weight, heads_all, preferred_element_type=F32)
    return (mixed.astype(F32) + update).astype(BF16)


def solution(mesh):
    in_specs = (
        P("head", "seq"),
        P(None, None, "seq"),
        P(None, "seq"),
        P(None, None, "head", None),
        P(None, None, "head", None),
        P(None, "head", None),
        P("seq"),
    )
    return jax.shard_map(
        functools.partial(body, mesh.shape["head"], math.isqrt(mesh.shape["seq"] // 2)),
        mesh=mesh,
        in_specs=in_specs,
        out_specs=P("head", "seq"),
        check_vma=False,
    )
```

```python
import functools
import math

import jax
import jax.numpy as jnp
from jax import lax
from jax.experimental import pallas as pl
from jax.experimental.pallas import tpu as pltpu
from jax.sharding import PartitionSpec as P

HD = 16
REACH = 256
TAPS = 27
CAP = 16
LANES = 128
MESH = pl.DeviceIdType.MESH
BF16 = jnp.bfloat16
F32 = jnp.float32


def remote(src, dst, send, recv, s, h):
    return pltpu.make_async_remote_copy(
        src_ref=src,
        dst_ref=dst,
        send_sem=send,
        recv_sem=recv,
        device_id=(s, h),
        device_id_type=MESH,
    )


def kernel(
    x,
    nbr,
    valid,
    cw,
    aw,
    pw,
    place,
    out,
    tables,
    mixes,
    heads_out,
    nb,
    vm,
    w,
    a,
    p,
    pq,
    pall,
    pt,
    y,
    kt,
    qm,
    va,
    places,
    pv,
    feats,
    tri,
    onehot,
    side_of,
    turned_feats,
    partial,
    going,
    come,
    land,
    flat,
    found,
    turned,
    moved,
    local,
    s1,
    r1,
    s2,
    r2,
    s3,
    r3,
    s4,
    r4,
    s5,
    r5,
    s6,
    r6,
    s7,
    r7,
    s8,
    r8,
    s9,
    r9,
    s10,
    r10,
):
    width, rows = out.shape
    heads = width // HD
    groups = lax.axis_size("head")
    shards = lax.axis_size("seq")
    side = places.shape[0]
    chips = side * side
    lines = 2 * places.shape[3]
    blocks = rows // REACH
    bits = rows.bit_length() - 1
    s = lax.axis_index("seq")
    h = lax.axis_index("head")
    core = lax.rem(s, 2)
    chip = s // 2
    zz = chip // side
    yy = lax.rem(chip, side)
    sibling = s + 1 - 2 * core
    after = lax.rem(s + 1, shards)
    before = lax.rem(s + shards - 1, shards)
    peers = [lax.rem(h + d, groups) for d in range(1, groups)]
    froms = [lax.rem(h + groups - d, groups) for d in range(1, groups)]
    sends = []

    def part(index, size=width, extra=0):
        return pl.ds(pl.multiple_of(index * width + extra, 16), size)

    mine = part(h)

    def ship(copy):
        copy.start()
        sends.append(copy)

    barrier = pltpu.get_barrier_semaphore()

    def greet(i, carry):
        other = lax.rem(chip + i, chips) * 2 + core
        pl.semaphore_signal(barrier, inc=1, device_id=(other, h), device_id_type=MESH)
        return carry

    for other in peers:
        pl.semaphore_signal(barrier, inc=1, device_id=(s, other), device_id_type=MESH)
    for other in (before, after):
        pl.semaphore_signal(barrier, inc=1, device_id=(other, h), device_id_type=MESH)
    loads = [
        pltpu.make_async_copy(x, tables.at[0, mine, pl.ds(REACH, rows)], local.at[0]),
        pltpu.make_async_copy(cw, w, local.at[1]),
        pltpu.make_async_copy(nbr, nb, local.at[2]),
        pltpu.make_async_copy(valid, vm, local.at[3]),
        pltpu.make_async_copy(aw, a, local.at[4]),
        pltpu.make_async_copy(pw, p, local.at[5]),
        pltpu.make_async_copy(place, places.at[zz, yy, core], local.at[6]),
    ]
    for load in loads:
        load.start()
    lax.fori_loop(1, chips, greet, 0, unroll=7)
    pl.semaphore_wait(barrier, chips - 1 + groups - 1 + 2)

    def gather_piece(b, source, j):
        for d, other in enumerate(peers):
            span = pl.ds(REACH + j * REACH, REACH)
            ship(
                remote(
                    source.at[:, pl.ds(j * REACH, REACH)],
                    tables.at[b, mine, span],
                    s1.at[b, j, d],
                    r1.at[b, j, d],
                    s,
                    other,
                )
            )

    def gather_wait(b, j):
        for d, other in enumerate(froms):
            theirs = tables.at[b, part(other), pl.ds(REACH + j * REACH, REACH)]
            remote(theirs, theirs, s1.at[b, j, d], r1.at[b, j, d], s, other).wait_recv()

    def places_along_z():
        for d in range(1, side):
            other = (lax.rem(zz + d, side) * side + yy) * 2 + core
            ship(remote(place, places.at[zz, yy, core], s6.at[d - 1], r6.at[d - 1], other, h))

    def places_along_y():
        loads[6].wait()
        for d in range(1, side):
            theirs = places.at[lax.rem(zz + side - d, side), yy, core]
            remote(theirs, theirs, s6.at[d - 1], r6.at[d - 1], s, h).wait_recv()
        for d in range(1, side):
            other = (zz * side + lax.rem(yy + d, side)) * 2 + core
            column = places.at[:, yy, core]
            ship(remote(column, column, s7.at[d - 1], r7.at[d - 1], other, h))

    def places_across():
        for d in range(1, side):
            theirs = places.at[:, lax.rem(yy + side - d, side), core]
            remote(theirs, theirs, s7.at[d - 1], r7.at[d - 1], s, h).wait_recv()
        column = places.at[:, :, core]
        ship(remote(column, column, s8.at[0], r8.at[0], sibling, h))

    def places_finish():
        theirs = places.at[:, :, 1 - core]
        remote(theirs, theirs, s8.at[0], r8.at[0], sibling, h).wait_recv()
        for line in range(lines):
            pltpu.make_async_copy(
                places.at[:, :, line // (lines // 2), line % (lines // 2)], pv.at[line], local.at[7]
            ).start()

    def weights_start():
        loads[5].wait()
        both = jnp.concatenate([p[0], p[1]], axis=0).astype(F32)
        pq[...] = both.T.astype(BF16)
        for d, other in enumerate(peers):
            ship(remote(pq.at[part(other), :], pall.at[h], s5.at[d], r5.at[d], s, other))
        pall[h] = pq[mine, :]

    def weights_finish():
        for d, other in enumerate(froms):
            remote(pall.at[other], pall.at[other], s5.at[d], r5.at[d], s, other).wait_recv()
        for b in range(2):
            span = slice(b * width, (b + 1) * width)
            pt[b] = jnp.concatenate([pall[g, :, span].astype(F32) for g in range(groups)], axis=1).astype(BF16)

    batch = 16
    strip = batch * CAP
    strips = chips // batch

    def prepare():
        weights_finish()
        places_finish()
        column = lax.broadcasted_iota(jnp.int32, (chips, LANES), 0)
        run = jnp.zeros((chips, 1), F32)
        half = lines // 2
        slots = []
        for line in range(lines):
            row = places[zz, yy, line // half, line % half : line % half + 1, :]
            device = row >> bits
            mask = jnp.where(device == column * 2 + core, 1.0, 0.0)
            counts = jnp.dot(mask.astype(BF16), tri[...], preferred_element_type=F32) + run
            run = counts[:, LANES - 1 :]
            rank = (jnp.sum(mask * counts, axis=0, keepdims=True) - 1.0).astype(jnp.int32)
            here = (device & 1) == core
            target = (device >> 1) * CAP + (rank & (CAP - 1))
            slots.append((jnp.where(here, target, -1), rank >> 4))
        spot = lax.broadcasted_iota(jnp.int32, (strip, rows), 0)
        for c in range(2):
            targets = jnp.concatenate([t for t, _ in slots[c * half : (c + 1) * half]], axis=1)
            halves = jnp.concatenate([e for _, e in slots[c * half : (c + 1) * half]], axis=1)
            side_of[c : c + 1, :] = halves
            for i in range(strips):
                rows_of = slice(i * strip, (i + 1) * strip)
                onehot[c, rows_of, :] = (spot == targets - i * strip).astype(F32).astype(BF16)

    def run_block(b):
        table = tables.at[b]
        mix = mixes.at[b]
        ho = heads_out.at[b]
        gather_wait(b, 0)
        first = remote(
            table.at[:, pl.ds(REACH, REACH)],
            table.at[:, pl.ds(REACH + rows, REACH)],
            s2.at[b, 0],
            r2.at[b, 0],
            before,
            h,
        )
        ship(first)
        if b == 0:
            places_along_y()
            for load in loads[1:5]:
                load.wait()
        taps = w[b].reshape(TAPS * width, -1)

        def products(tile):
            points = table[:, tile * REACH : (tile + 1) * REACH]
            value = jnp.dot(taps, points, preferred_element_type=F32).astype(BF16)
            y[:, tile] = value.reshape(TAPS, width, REACH)

        def conv(blk):
            cols = slice(blk * REACH, (blk + 1) * REACH)
            base = s * rows + (blk - 1) * REACH
            total = jnp.zeros((width, REACH), F32)
            for t in range(TAPS):
                index = nb[t, b : b + 1, cols]
                spot = index - base
                tile = jnp.where(index < 0, 3, spot >> 8)
                within = (spot & (REACH - 1)).astype(F32).astype(BF16)
                chosen = jnp.where(position == within, one, zero)
                terms = y[t, blk : blk + 3].reshape(3 * width, REACH)
                picked = jnp.dot(terms, chosen, preferred_element_type=F32)
                term = jnp.where(tile == 0, picked[:width], 0.0)
                term = jnp.where(tile == 1, picked[width : 2 * width], term)
                term = jnp.where(tile == 2, picked[2 * width :], term)
                total = total + term
            own = table[mine, REACH + blk * REACH : REACH + (blk + 1) * REACH].astype(F32)
            mix[mine, cols] = (own + total).astype(BF16)
            for d, other in enumerate(peers):
                ship(remote(mix.at[mine, cols], mix.at[mine, cols], s3.at[b, blk, d], r3.at[b, blk, d], s, other))

        products(1)
        for tile in range(2, blocks):
            gather_wait(b, tile - 1)
            products(tile)
        conv(1)
        gather_wait(b, blocks - 1)
        last = remote(
            table.at[:, pl.ds(rows, REACH)],
            table.at[:, pl.ds(0, REACH)],
            s2.at[b, 1],
            r2.at[b, 1],
            after,
            h,
        )
        ship(last)
        products(blocks)
        for blk in range(2, blocks - 1):
            conv(blk)
        if b == 0:
            places_across()
        first.wait_recv()
        products(blocks + 1)
        conv(blocks - 1)
        last.wait_recv()
        products(0)
        conv(0)

        scale = 1.0 / HD**0.5
        bias = jnp.where(vm[b : b + 1, :] > 0, 0.0, -1e30)
        weights = a[b].reshape(3 * width, -1)
        for blk in (*range(1, blocks), 0):
            cols = slice(blk * REACH, (blk + 1) * REACH)
            for d, other in enumerate(froms):
                theirs = mix.at[part(other), cols]
                remote(theirs, theirs, s3.at[b, blk, d], r3.at[b, blk, d], s, other).wait_recv()
            values = mix[:, cols].astype(F32)
            centred = values - jnp.mean(values, axis=0, keepdims=True)
            variance = jnp.mean(centred * centred, axis=0, keepdims=True)
            normed = (centred * lax.rsqrt(variance + 1e-05)).astype(BF16)
            qkv = jnp.dot(weights, normed, preferred_element_type=F32)
            query = (qkv[:width].astype(BF16).astype(F32) * scale).astype(BF16)
            value = qkv[2 * width :].astype(BF16)
            for hd in range(heads):
                span = slice(hd * HD, (hd + 1) * HD)
                qm[hd, span, cols] = query[span]
                va[hd, :HD, cols] = value[span]
            tail = jnp.where(
                lax.broadcasted_iota(jnp.int32, (width, REACH), 0) == 0, bias[:, cols], 0.0
            )
            keys = jnp.concatenate([qkv[width : 2 * width], tail], axis=0)
            kt[cols, :] = keys.T.astype(BF16)

        def score(hd):
            return jnp.dot(kt[...], qm[hd], preferred_element_type=F32)

        upcoming = score(0)
        for hd in range(heads):
            scores = upcoming
            if hd + 1 < heads:
                upcoming = score(hd + 1)
            top = jnp.max(scores, axis=0, keepdims=True)
            probs = jnp.exp(scores - top).astype(BF16)
            summed = jnp.dot(va[hd], probs, preferred_element_type=F32)
            result = summed[:HD] / summed[HD : HD + 1]
            span = part(h, HD, hd * HD)
            ho[span, :] = result.astype(BF16)
            for d, other in enumerate(peers):
                ship(remote(ho.at[span, :], ho.at[span, :], s4.at[b, hd, d], r4.at[b, hd, d], s, other))

    def project(b):
        mix = mixes.at[b]
        ho = heads_out.at[b]
        for hd in range(heads):
            for d, other in enumerate(froms):
                theirs = ho.at[part(other, HD, hd * HD), :]
                remote(theirs, theirs, s4.at[b, hd, d], r4.at[b, hd, d], s, other).wait_recv()
        update = jnp.dot(pt[b], ho[...], preferred_element_type=F32)
        return (mix[mine, :].astype(F32) + update).astype(BF16)

    for j in range(blocks):
        gather_piece(0, x, j)
    places_along_z()
    low = lax.broadcasted_iota(jnp.int32, (LANES, LANES), 0)
    high = lax.broadcasted_iota(jnp.int32, (LANES, LANES), 1)
    tri[...] = jnp.where(low <= high, 1.0, 0.0).astype(BF16)
    position = lax.broadcasted_iota(jnp.int32, (REACH, REACH), 0).astype(F32).astype(BF16)
    one, zero = jnp.ones((), BF16), jnp.zeros((), BF16)
    ones = jnp.where(lax.broadcasted_iota(jnp.int32, (HD, rows), 0) == 0, 1.0, 0.0).astype(BF16)
    qm[...] = jnp.zeros(qm.shape, BF16)
    for hd in range(heads):
        qm[hd, width : width + HD, :] = ones
        va[hd, HD:, :] = ones
    weights_start()
    loads[0].wait()
    run_block(0)
    prepare()

    feats[core] = project(0)
    swap = remote(feats.at[core], feats.at[core], s9.at[0], r9.at[0], sibling, h)
    ship(swap)
    own = chip // batch

    def turn_points(c):
        points = feats[c].astype(F32)
        half_of = side_of[pl.ds(c, 1), :]
        both = jnp.concatenate([jnp.where(half_of == e, points, 0.0) for e in range(2)], axis=0)
        turned_feats[c] = both.T.astype(BF16)

    def sorted_part(c, which):
        span = pl.ds(pl.multiple_of(which * strip, strip), strip)
        return span, jnp.dot(onehot[c, span, :], turned_feats[c], preferred_element_type=F32)

    def sort_own(which, carry):
        span, value = sorted_part(core, which)
        partial[span, :] = value
        return carry

    turn_points(core)
    lax.fori_loop(0, strips, sort_own, 0, unroll=2)
    theirs = feats.at[1 - core]
    remote(theirs, theirs, s9.at[0], r9.at[0], sibling, h).wait_recv()
    turn_points(1 - core)

    def sort(i, carry):
        which = lax.rem(own + i, strips)
        span, value = sorted_part(1 - core, which)
        both = (partial[span, :] + value).astype(BF16)
        going[pl.ds(which * batch, batch)] = both.reshape(batch, CAP, 2 * width)

        def send(j, c):
            other = which * batch + lax.rem(chip + j, batch)

            @pl.when(other != chip)
            def _():
                remote(going.at[other], come.at[chip], s10.at[0], r10.at[0], other * 2 + core, h).start()

            return c

        lax.fori_loop(0, batch, send, 0)
        return carry

    lax.fori_loop(0, strips, sort, 0)
    stay = pltpu.make_async_copy(going.at[chip], come.at[chip], local.at[8])
    stay.start()

    pltpu.make_async_copy(pv, pv, local.at[7]).wait()
    run = jnp.zeros((chips, 1), F32)
    for line in range(lines):
        row = pv[line].reshape(chips, LANES)
        mask = jnp.where((row >> bits) == s, 1.0, 0.0)
        counts = jnp.dot(mask.astype(BF16), tri[...], preferred_element_type=F32) + run
        run = counts[:, LANES - 1 :]
        land[line] = jnp.where(mask > 0, counts - 1.0, -1.0)
        flat[line] = ((row & (rows - 1)) + 1).astype(F32)
    for start in range(0, chips, 8):
        ranks = [land[line, start : start + 8, :] for line in range(lines)]
        spots = [flat[line, start : start + 8, :] for line in range(lines)]

        def settle(k, carry):
            rank = k.astype(F32)
            total = jnp.zeros((8, LANES), F32)
            for line in range(lines):
                total += jnp.where(ranks[line] == rank, spots[line], 0.0)
            where = jnp.sum(total, axis=1, keepdims=True)
            found[pl.ds(pl.multiple_of(k * chips + start, 8), 8), :] = jnp.broadcast_to(where, (8, LANES))
            return carry

        lax.fori_loop(0, 2 * CAP, settle, 0, unroll=8)
    lane = lax.broadcasted_iota(jnp.int32, (chips, LANES), 1).astype(F32) + 1.0

    def turn(k, carry):
        span = pl.ds(pl.multiple_of(k * chips, 16), chips)
        spots = found[span, :]
        for start in range(0, rows, LANES):
            turned[span, start : start + LANES] = (spots == lane + float(start)).astype(F32).astype(BF16)
        return carry

    lax.fori_loop(0, 2 * CAP, turn, 0, unroll=2)

    stay.wait()
    many = pl.ds(0, chips - 1)
    every = remote(going.at[many], come.at[many], s10.at[0], r10.at[0], sibling, h)
    every.wait_recv()
    arrived = come[...].astype(F32)
    parts = []
    for k in range(0, CAP, 2):
        two = jnp.concatenate([arrived[:, k, :], arrived[:, k + 1, :]], axis=0)
        parts.append(two.T.astype(BF16))
    packed = jnp.concatenate(parts, axis=1)
    half = CAP * chips
    for j in range(blocks):
        cols = slice(j * REACH, (j + 1) * REACH)
        total = jnp.dot(packed[:width], turned[:half, cols], preferred_element_type=F32)
        total += jnp.dot(packed[width:], turned[half:, cols], preferred_element_type=F32)
        moved[:, cols] = total.astype(BF16)
        gather_piece(1, moved, j)
    tables[1, mine, REACH : REACH + rows] = moved[...]
    run_block(1)
    out[...] = project(1)
    for copy in sends:
        copy.wait_send()
    every.wait_send()


def body(groups, side, features, neighbours, valid, conv_weight, attn_weight, proj_weight, hilbert_place):
    width, rows = features.shape
    channels = width * groups
    heads = width // HD
    blocks = rows // REACH
    chips = side * side
    lines = 2 * rows // LANES
    others = groups - 1
    dma = pltpu.SemaphoreType.DMA
    vmem = pltpu.VMEM
    pairs = [(2, blocks, others), (2, 2), (2, blocks, others), (2, heads, others), (others,)]
    pairs += [(side - 1,), (side - 1,), (1,), (1,), (1,)]
    return pl.pallas_call(
        kernel,
        out_shape=jax.ShapeDtypeStruct((width, rows), BF16),
        in_specs=[pl.BlockSpec(memory_space=pl.ANY)] * 7,
        out_specs=pl.BlockSpec(memory_space=pltpu.VMEM),
        scratch_shapes=[
            vmem((2, channels, rows + 2 * REACH), BF16),
            vmem((2, channels, rows), BF16),
            vmem((2, channels, rows), BF16),
            vmem((TAPS, 2, rows), jnp.int32),
            vmem((2, rows), jnp.int32),
            vmem((2, TAPS, width, channels), BF16),
            vmem((2, 3, width, channels), BF16),
            vmem((2, width, channels), BF16),
            vmem((channels, 2 * width), BF16),
            vmem((groups, width, 2 * width), BF16),
            vmem((2, width, channels), BF16),
            vmem((TAPS, blocks + 2, width, REACH), BF16),
            vmem((rows, 2 * width), BF16),
            vmem((heads, 2 * width, rows), BF16),
            vmem((heads, 2 * HD, rows), BF16),
            vmem((side, side, 2, rows // LANES, LANES), jnp.int32),
            vmem((lines, side, side, LANES), jnp.int32),
            vmem((2, width, rows), BF16),
            vmem((LANES, LANES), BF16),
            vmem((2, chips * CAP, rows), BF16),
            vmem((2, rows), jnp.int32),
            vmem((2, rows, 2 * width), BF16),
            vmem((chips * CAP, 2 * width), F32),
            vmem((chips, CAP, 2 * width), BF16),
            vmem((chips, CAP, 2 * width), BF16),
            vmem((lines, chips, LANES), F32),
            vmem((lines, chips, LANES), F32),
            vmem((2 * CAP * chips, LANES), F32),
            vmem((2 * CAP * chips, rows), BF16),
            vmem((width, rows), BF16),
            dma((9,)),
            *[dma(shape) for shape in pairs for _ in range(2)],
        ],
        compiler_params=pltpu.CompilerParams(
            collective_id=0, has_side_effects=True, vmem_limit_bytes=60 * 2**20
        ),
        name="blocks",
    )(
        features,
        jnp.swapaxes(neighbours, 0, 1),
        valid,
        conv_weight,
        attn_weight,
        proj_weight,
        hilbert_place.reshape(rows // LANES, LANES),
    )


def solution(mesh):
    in_specs = (
        P("head", "seq"),
        P(None, None, "seq"),
        P(None, "seq"),
        P(None, None, "head", None),
        P(None, None, "head", None),
        P(None, "head", None),
        P("seq"),
    )
    return jax.shard_map(
        functools.partial(body, mesh.shape["head"], math.isqrt(mesh.shape["seq"] // 2)),
        mesh=mesh,
        in_specs=in_specs,
        out_specs=P("head", "seq"),
        check_vma=False,
    )
```
